256 devices in a mesh: section: 4 (over y), dp: 64 (over z, x, core).
Axes of the slice: x: 4, y: 4, z: 8, core: 2. Of those that a mesh axis runs over, the one named last changes fastest.
Arguments:
- layer_inputs: bfloat16 [4, 8192, 8192], P('section', 'dp'), may hold values from -6 to 6
- top_grad: bfloat16 [8192, 8192], P('dp'), may hold values from -6 to 6
- tenant_ids: int32 [8192], P('dp'), may hold values from 0 to 7
- owner_map: int32 [8], replicated, may hold values from 0 to 63, as said below
- frozen: bfloat16 [4, 8192, 1024], P('section', 'dp'), may hold values from -0.0625 to 0.0625
- adapt_a: bfloat16 [4, 8192, 128], P('section', 'dp'), may hold values from -0.0625 to 0.0625
- adapt_b: bfloat16 [4, 128, 512], P('section'), may hold values from -0.25 to 0.25
Outputs:
- grads_in: bfloat16 [4, 8192, 8192], P('section', 'dp')
- owned_a: float32 [4, 64, 16, 8192], P('section', 'dp')
- owned_b: float32 [4, 64, 16, 512], P('section', 'dp')
The draws below stay inside these ranges and needn't reach their ends.
Inputs may be any that keep to these rules, and one draw needn't show every extreme that they name: `owner_map`: distinct owners for distinct tenants.
All inputs are finite; a program needn't handle non-finite values.
Results may differ from the reference program's by a relative error of at most 0.011.
Values may be sent and summed in bfloat16 or wider, within the bound.
A program may use at most 192 MiB of HBM per device.

```python
import math
import jax
import jax.numpy as jnp
import numpy as np
from jax import lax

D = 8192
KV = 512
RANK = 16
TENANTS = 8
TOKENS = 8192
SECTIONS = 4
TR = 128
N_DP = 64


def draw_owner_map(key, part):
    key = jax.random.fold_in(key, 7)
    return jax.random.permutation(key, jnp.arange(N_DP, dtype=jnp.int32))[:TENANTS].astype(jnp.int32)


def with_ends(array, key, smallest, top_value):
    longest = array.shape.index(max(array.shape))
    spots = []
    for shift in (0, 1):
        where = [jax.random.randint(jax.random.fold_in(key, axis), (), 0, length) for axis, length in enumerate(array.shape)]
        where[longest] = (where[longest] + shift) % array.shape[longest]
        spots.append(tuple(where))
    return array.at[spots[0]].set(smallest).at[spots[1]].set(top_value)


def block_scale(stream_key, shape, cuts, smallest, largest):
    def one(position, blocks):
        draws = jax.random.uniform(jax.random.fold_in(jax.random.fold_in(stream_key, 6), position), (blocks,), jnp.float32, smallest / len(cuts), largest / len(cuts))
        return jnp.repeat(jnp.exp(draws), shape[position] // blocks).reshape((-1,) + (1,) * (len(shape) - position - 1))

    loudness = one(*cuts[0])
    for cut in cuts[1:]:
        loudness = loudness * one(*cut)
    return loudness


def cumulative_ranks(amount, slope):
    loads = [(1 << 20) // math.isqrt(grade ** slope) + 1 for grade in range(1, amount + 1)]
    deviation = 1 + sum(loads) // (1 << 30)
    return np.cumsum(np.array([max(1, weight // deviation) for weight in loads]))


def skewed_ids(key, extent, amount, skew):
    grid = cumulative_ranks(amount, skew)
    lot = jax.random.randint(jax.random.fold_in(key, 1), extent, 0, int(grid[amount - 1]))
    rank = jnp.searchsorted(jnp.asarray(grid, jnp.int32), lot, side="right")
    return jax.random.permutation(jax.random.fold_in(key, 2), amount)[rank].astype(jnp.int32)


def centred(stream_key, extent, deviation, most, shards=(), held_as=jnp.bfloat16):
    entries = deviation * jax.random.normal(stream_key, extent, jnp.float32)
    if shards:
        entries = entries * block_scale(stream_key, extent, shards, -0.22, 0.18)
    return jnp.clip(entries, -most, most).astype(held_as)


def setup_inputs(seed: int = 0) -> dict:
    splits = jax.random.split(jax.random.key(seed), 8)
    return {
        "layer_inputs": centred(splits[0], (SECTIONS, TOKENS, D), 1.0, 6.0, ((0, 4), (1, 64))),
        "top_grad": centred(splits[1], (TOKENS, D), 1.0, 6.0, ((0, 64),)),
        "tenant_ids": with_ends(skewed_ids(splits[2], (TOKENS,), TENANTS, 2), jax.random.fold_in(splits[2], 3), 0, TENANTS - 1).astype(jnp.int32),
        "owner_map": draw_owner_map(jax.random.fold_in(splits[7], 71), 0),
        "frozen": centred(splits[4], (SECTIONS, D, 2 * KV), D ** -0.5, 0.0625, ((0, 4), (1, 64))),
        "adapt_a": centred(splits[5], (SECTIONS, D, TR), D ** -0.5, 0.0625, ((0, 4), (1, 64))),
        "adapt_b": centred(splits[6], (SECTIONS, TR, KV), KV ** -0.5, 0.25, ((0, 4),)),
    }


def reference(layer_inputs, top_grad, tenant_ids, owner_map, frozen, adapt_a, adapt_b):
    scale = 2.0
    columns = jnp.arange(TR, dtype=jnp.int32) // RANK
    mask = (columns[None, :] == tenant_ids[:, None]).astype(jnp.float32)
    select = (owner_map[None, :] == jnp.arange(N_DP, dtype=jnp.int32)[:, None]).astype(jnp.float32)
    grad = top_grad
    grads_list = [None] * SECTIONS
    owned_a_list = [None] * SECTIONS
    owned_b_list = [None] * SECTIONS
    for section in reversed(range(SECTIONS)):
        inputs = layer_inputs[section]
        w_value = frozen[section][:, :KV]
        out_t = frozen[section][:, KV:]
        down = adapt_a[section]
        upmap = adapt_b[section]
        value_grad = jnp.dot(grad, out_t, preferred_element_type=jnp.float32).astype(jnp.bfloat16)
        low = (mask * jnp.dot(inputs, down, preferred_element_type=jnp.float32)).astype(jnp.bfloat16)
        back = (mask * lax.dot_general(value_grad, upmap, (((1,), (1,)), ((), ())), preferred_element_type=jnp.float32)).astype(jnp.bfloat16)
        total = grad.astype(jnp.float32) + lax.dot_general(value_grad, w_value, (((1,), (1,)), ((), ())), preferred_element_type=jnp.float32)
        total = total + scale * lax.dot_general(back, down, (((1,), (1,)), ((), ())), preferred_element_type=jnp.float32)
        grad_in = total.astype(jnp.bfloat16)
        grad_a = scale * lax.dot_general(inputs, back, (((0,), (0,)), ((), ())), preferred_element_type=jnp.float32)
        grad_b = scale * lax.dot_general(low, value_grad, (((0,), (0,)), ((), ())), preferred_element_type=jnp.float32)
        owned_a_list[section] = jnp.einsum("jt,dtr->jrd", select, grad_a.reshape(D, TENANTS, RANK), precision=lax.Precision.HIGHEST)
        owned_b_list[section] = jnp.einsum("jt,trk->jrk", select, grad_b.reshape(TENANTS, RANK, KV), precision=lax.Precision.HIGHEST)
        grads_list[section] = grad_in
        grad = grad_in
    return jnp.stack(grads_list), jnp.stack(owned_a_list), jnp.stack(owned_b_list)
```

```python
import functools

import jax
import jax.numpy as jnp
from jax import lax
from jax.experimental import pallas as pl
from jax.experimental.pallas import tpu as pltpu
from jax.sharding import PartitionSpec as P

MESH = pl.DeviceIdType.MESH
NY, NZ, NX, NC = 4, 8, 4, 2
D = 8192
KV = 512
TR = 128
RANK = 16
WA = KV + TR
ROWS = 128
SUB = ROWS // NY
COLS = NZ * NX * SUB


def mm(a, b):
    return lax.dot_general(a, b, (((1,), (0,)), ((), ())), preferred_element_type=jnp.float32)


def mm_t(a, b):
    return lax.dot_general(a, b, (((1,), (1,)), ((), ())), preferred_element_type=jnp.float32)


def chain_kernel(
    g0_ref, fz_ref, aa_ref, bb_ref, ids_ref,
    out_ref, vb_ref,
    ob, wab, gall, rbuf, g0v, gsend, pb, rsr, vball, bbuf, perm,
    ring_s, ring_r, y_s, yo_r, yw_r, b_r, g_sem, sib_sem, rs_s, rs_r, vb_s, vb_r, out_s, out_r,
):
    y = lax.axis_index("section")
    d = lax.axis_index("dp")
    z = d // (NX * NC)
    x = (d // NC) % NX
    c = d % NC

    def dev(yy, zz, xx, cc):
        return (yy, zz * (NX * NC) + xx * NC + cc)

    xr, xl = (x + 1) % NX, (x + NX - 1) % NX
    xo = (x + 2) % NX
    zr, zl = (z + 1) % NZ, (z + NZ - 1) % NZ
    sib = 1 - c
    pending = []

    def send(src, dst, ssem, rsem, device):
        copy = pltpu.make_async_remote_copy(
            src_ref=src, dst_ref=dst, send_sem=ssem, recv_sem=rsem,
            device_id=device, device_id_type=MESH,
        )
        copy.start()
        pending.append(copy)

    def landed(dst, rsem):
        pltpu.make_async_copy(dst, dst, rsem).wait()

    load = pltpu.make_async_copy(g0_ref, g0v, g_sem)
    load.start()

    column = [
        (dq, dc, (y + dq) % NY, (c + dc) % NC)
        for dq in range(NY) for dc in range(NC) if dq or dc
    ]
    barrier = pltpu.get_barrier_semaphore()
    for _, _, yy, cc in column:
        pl.semaphore_signal(barrier, inc=1, device_id=dev(yy, z, x, cc), device_id_type=MESH)
    for zz, xx in ((z, xr), (z, xl), (zr, x), (zl, x)):
        pl.semaphore_signal(barrier, inc=1, device_id=dev(y, zz, xx, c), device_id_type=MESH)
    pl.semaphore_wait(barrier, 11)

    local = []
    for dq in range(NY):
        yy = (y + dq) % NY
        rows = pl.ds(pl.multiple_of(yy * SUB, SUB), SUB)
        parts = (
            (fz_ref.at[rows, pl.ds(KV, KV)], ob.at[y, z, x], yo_r.at[y]),
            (fz_ref.at[rows, pl.ds(0, KV)], wab.at[y, z, x, :, pl.ds(0, KV)], yw_r.at[y]),
            (aa_ref.at[rows, :], wab.at[y, z, x, :, pl.ds(KV, TR)], yw_r.at[y]),
            (bb_ref, bbuf.at[y], b_r.at[y]),
        )
        for i, (src, dst, rsem) in enumerate(parts):
            if dq:
                send(src, dst, y_s.at[dq, i], rsem, dev(yy, z, x, c))
            else:
                copy = pltpu.make_async_copy(src, dst, rsem)
                copy.start()

    half = SUB // 2

    def ring(piece, k):
        s = NY - 1 - piece // 2
        is_o = piece % 2 == 0
        buf = ob if is_o else wab
        width = KV if is_o else WA
        lo, hi = pl.ds(0, 256), pl.ds(256, width - 256)
        top, low = pl.ds(0, half), pl.ds(half, half)

        def step(part, stage, moves):
            for way, (src, dst) in enumerate(moves):
                zz, xx = dst
                send(src, src, ring_s.at[piece, part, stage, way],
                     ring_r.at[piece, part, stage, way], dev(y, zz, xx, c))

        def arrive(part, stage, refs):
            for way, ref in enumerate(refs):
                landed(ref, ring_r.at[piece, part, stage, way])

        def zb(by):
            return (z + by + NZ) % NZ

        right, left = (z, xr), (z, xl)
        up, down = (zr, x), (zl, x)
        a_recv = [
            (buf.at[s, z, xl, top], buf.at[s, z, xr, top]),
            (buf.at[s, z, xo, top, lo], buf.at[s, z, xo, top, hi]),
            (buf.at[s, zb(-1), :, top], buf.at[s, zb(1), :, top]),
            (buf.at[s, zb(-2), :, top], buf.at[s, zb(2), :, top]),
            (buf.at[s, zb(-3), :, top], buf.at[s, zb(3), :, top]),
            (buf.at[s, zb(4), pl.ds(0, 2), top], buf.at[s, zb(4), pl.ds(2, 2), top]),
        ]
        a_send = [
            ((buf.at[s, z, x, top], right), (buf.at[s, z, x, top], left)),
            ((buf.at[s, z, xl, top, lo], right), (buf.at[s, z, xr, top, hi], left)),
            ((buf.at[s, z, :, top], up), (buf.at[s, z, :, top], down)),
            ((buf.at[s, zb(-1), :, top], up), (buf.at[s, zb(1), :, top], down)),
            ((buf.at[s, zb(-2), :, top], up), (buf.at[s, zb(2), :, top], down)),
            ((buf.at[s, zb(-3), pl.ds(0, 2), top], up), (buf.at[s, zb(3), pl.ds(2, 2), top], down)),
        ]
        b_recv = [
            (buf.at[s, zb(-1), x, low], buf.at[s, zb(1), x, low]),
            (buf.at[s, zb(-2), x, low], buf.at[s, zb(2), x, low]),
            (buf.at[s, zb(-3), x, low], buf.at[s, zb(3), x, low]),
            (buf.at[s, zb(4), x, low, lo], buf.at[s, zb(4), x, low, hi]),
            (buf.at[s, :, xl, low], buf.at[s, :, xr, low]),
            (buf.at[s, pl.ds(0, 4), xo, low], buf.at[s, pl.ds(4, 4), xo, low]),
        ]
        b_send = [
            ((buf.at[s, z, x, low], up), (buf.at[s, z, x, low], down)),
            ((buf.at[s, zb(-1), x, low], up), (buf.at[s, zb(1), x, low], down)),
            ((buf.at[s, zb(-2), x, low], up), (buf.at[s, zb(2), x, low], down)),
            ((buf.at[s, zb(-3), x, low, lo], up), (buf.at[s, zb(3), x, low, hi], down)),
            ((buf.at[s, :, x, low], right), (buf.at[s, :, x, low], left)),
            ((buf.at[s, pl.ds(0, 4), xl, low], right), (buf.at[s, pl.ds(4, 4), xr, low], left)),
        ]
        if k == 0:
            landed(buf.at[s, z, x], (yo_r if is_o else yw_r).at[s])
        else:
            arrive(0, k - 1, a_recv[k - 1])
            arrive(1, k - 1, b_recv[k - 1])
        if k < 6:
            step(0, k, a_send[k])
            step(1, k, b_send[k])

    def compact():
        load.wait()
        source = lax.broadcasted_iota(jnp.int32, (NX * NC * ROWS, ROWS), 0)
        target = lax.broadcasted_iota(jnp.int32, (NX * NC * ROWS, ROWS), 1)
        base = (target // SUB) * (NC * ROWS) + target % SUB + y * SUB
        mine = (source == base + c * ROWS).astype(jnp.bfloat16)
        other = (source == base + sib * ROWS).astype(jnp.bfloat16)
        own = pl.ds(pl.multiple_of(c * ROWS, ROWS), ROWS)

        for zz in range(NZ):
            block = g0v[:, zz * 1024:(zz + 1) * 1024]
            gsend[:, zz * ROWS:(zz + 1) * ROWS] = mm(block, other).astype(jnp.bfloat16)
        send(gsend, gall.at[NY, own], sib_sem.at[0], sib_sem.at[1], dev(y, z, x, sib))
        for zz in range(NZ):
            block = g0v[:, zz * 1024:(zz + 1) * 1024]
            gall[NY, own, zz * ROWS:(zz + 1) * ROWS] = mm(block, mine).astype(jnp.bfloat16)
        landed(gsend, sib_sem.at[1])

        p_in = lax.broadcasted_iota(jnp.int32, (NY * ROWS, NY * ROWS), 0)
        p_out = lax.broadcasted_iota(jnp.int32, (NY * ROWS, NY * ROWS), 1)
        want = ((p_out // SUB) % NY) * ROWS + (p_out // ROWS) * SUB + p_out % SUB
        perm[...] = (p_in == want).astype(jnp.bfloat16)

    def block_of(yy, cc):
        return pl.ds(pl.multiple_of(cc * ROWS + yy * SUB, SUB), SUB)

    def partial(s):
        right = ob[s].reshape(COLS, KV)
        pb[s] = mm(gall[s + 1], right).astype(jnp.bfloat16)
        for dq, dc, yy, cc in column:
            j = dq * NC + dc
            send(pb.at[s, block_of(yy, cc)], rsr.at[s, j], rs_s.at[s, j], rs_r.at[s, j], dev(yy, z, x, cc))

    def finalise(s):
        total = pb[s, block_of(y, c), :].astype(jnp.float32)
        for dq, dc, _, _ in column:
            j = dq * NC + dc
            landed(rsr.at[s, j], rs_r.at[s, j])
            total = total + rsr[s, j].astype(jnp.float32)
        value = total.astype(jnp.bfloat16)
        landed(bbuf.at[s], b_r.at[s])
        ids = ids_ref[pl.ds(pl.multiple_of(y * SUB, SUB), SUB), :]
        columns = lax.broadcasted_iota(jnp.int32, (SUB, TR), 1) // RANK
        mask = (columns == ids).astype(jnp.float32)
        back = (mask * mm_t(value, bbuf[s])).astype(jnp.bfloat16)
        here = block_of(y, c)
        vball[s, here, 0:KV] = value
        vball[s, here, KV:WA] = (2.0 * back.astype(jnp.float32)).astype(jnp.bfloat16)
        for dq, dc, yy, cc in column:
            j = dq * NC + dc
            send(vball.at[s, here], vball.at[s, here], vb_s.at[s, j], vb_r.at[s, j], dev(yy, z, x, cc))

    def update(s):
        for dq, dc, _, _ in column:
            j = dq * NC + dc
            there = block_of((y - dq + NY) % NY, (c - dc + NC) % NC)
            landed(vball.at[s, there], vb_r.at[s, j])
        for i in range(4):
            cols = slice(i * 256, (i + 1) * 256)
            right = wab[s, 2 * i:2 * i + 2].reshape(256, WA)
            delta = mm_t(vball[s], right)
            gall[s, :, cols] = (gall[s + 1, :, cols].astype(jnp.float32) + delta).astype(jnp.bfloat16)
        own = pl.ds(pl.multiple_of(c * ROWS, ROWS), ROWS)
        others = pl.ds(pl.multiple_of(sib * ROWS, ROWS), ROWS)
        dq = (s - y + NY) % NY
        send(gall.at[s, others], rbuf.at[y, c], out_s.at[s, 1], out_r.at[dq * 2 + 1], dev(s, z, x, sib))
        direct = pltpu.make_async_remote_copy(
            src_ref=gall.at[s, own], dst_ref=rbuf.at[y, c], send_sem=out_s.at[s, 0], recv_sem=out_r.at[dq * 2],
            device_id=dev(s, z, x, c), device_id_type=MESH,
        )
        keep = pltpu.make_async_copy(gall.at[s, own], rbuf.at[y, c], out_r.at[0])

        @pl.when(y != s)
        def _():
            direct.start()

        @pl.when(y == s)
        def _():
            keep.start()

    compact()
    for t in range(15):
        for piece in range(8):
            if 0 <= t - piece <= 6:
                ring(piece, t - piece)
        if t >= 6 and t % 2 == 0:
            i = (t - 6) // 2
            if i > 0:
                update(NY - i)
            if i < NY:
                partial(NY - 1 - i)
        elif t >= 7:
            finalise(NY - 1 - (t - 7) // 2)

    vb_ref[...] = vball[y, pl.ds(pl.multiple_of(c * ROWS, ROWS), ROWS), :]
    for j in range(NY * NC):
        landed(rbuf.at[(y - j // 2 + NY) % NY, (c - j % 2 + NC) % NC], out_r.at[j])
    for zz in range(NZ):
        for cc in range(NC):
            block = jnp.concatenate([rbuf[q, cc, :, zz * ROWS:(zz + 1) * ROWS] for q in range(NY)], axis=1)
            mixed = mm(block, perm[...]).astype(jnp.bfloat16)
            for xx in range(NX):
                at = zz * 1024 + xx * 256 + cc * ROWS
                out_ref[:, at:at + ROWS] = mixed[:, xx * ROWS:(xx + 1) * ROWS]

    for s in range(NY):
        @pl.when(y != s)
        def _(s=s):
            own = pl.ds(pl.multiple_of(c * ROWS, ROWS), ROWS)
            pltpu.make_async_copy(gall.at[s, own], gall.at[s, own], out_s.at[s, 0]).wait()
    for copy in pending:
        copy.wait_send()


def chain(g0, fz, aa, bb, ids):
    vmem = pl.BlockSpec(memory_space=pltpu.VMEM)
    dma = pltpu.SemaphoreType.DMA
    bf = jnp.bfloat16
    return pl.pallas_call(
        chain_kernel,
        out_shape=(
            jax.ShapeDtypeStruct((ROWS, D), bf),
            jax.ShapeDtypeStruct((ROWS, WA), bf),
        ),
        in_specs=[pl.BlockSpec(memory_space=pl.ANY), vmem, vmem, vmem, vmem],
        out_specs=(vmem, vmem),
        scratch_shapes=[
            pltpu.VMEM((NY, NZ, NX, SUB, KV), bf),
            pltpu.VMEM((NY, NZ, NX, SUB, WA), bf),
            pltpu.VMEM((NY + 1, NC * ROWS, COLS), bf),
            pltpu.VMEM((NY, NC, ROWS, COLS), bf),
            pltpu.VMEM((ROWS, D), bf),
            pltpu.VMEM((ROWS, COLS), bf),
            pltpu.VMEM((NY, NC * ROWS, KV), bf),
            pltpu.VMEM((NY, NY * NC, SUB, KV), bf),
            pltpu.VMEM((NY, NC * ROWS, WA), bf),
            pltpu.VMEM((NY, TR, KV), bf),
            pltpu.VMEM((NY * ROWS, NY * ROWS), bf),
            dma((8, 2, 6, 2)),
            dma((8, 2, 6, 2)),
            dma((NY, 4)),
            dma((NY,)),
            dma((NY,)),
            dma((NY,)),
            dma,
            dma((2,)),
            dma((NY, NY * NC)),
            dma((NY, NY * NC)),
            dma((NY, NY * NC)),
            dma((NY, NY * NC)),
            dma((NY, 2)),
            dma((NY * NC,)),
        ],
        compiler_params=pltpu.CompilerParams(
            collective_id=0, has_side_effects=True, vmem_limit_bytes=50 * 2**20
        ),
        cost_estimate=pl.CostEstimate(flops=4 * 10**9, bytes_accessed=10**7, transcendentals=0),
    )(g0, fz, aa, bb, ids)


def body(layer_inputs, top_grad, tenant_ids, owner_map, frozen, adapt_a, adapt_b):
    my_data = lax.axis_index("dp")
    inputs = layer_inputs[0]
    down = lax.all_gather(adapt_a[0], "dp", axis=0, tiled=True)
    grads, vb = chain(top_grad, frozen[0], adapt_a[0], adapt_b[0], tenant_ids[:, None])
    values, back2 = vb[:, :KV], vb[:, KV:]
    columns = lax.broadcasted_iota(jnp.int32, (1, TR), 1) // RANK
    mask = (columns == tenant_ids[:, None]).astype(jnp.float32)
    low = (mask * mm(inputs, down)).astype(jnp.bfloat16)
    sum_a = lax.dot_general(back2, inputs, (((0,), (0,)), ((), ())), preferred_element_type=jnp.float32)
    sum_b = 2.0 * lax.dot_general(low, values, (((0,), (0,)), ((), ())), preferred_element_type=jnp.float32)
    full = lax.psum(jnp.concatenate([sum_a, sum_b], axis=1), "dp")
    owned = (owner_map == my_data).astype(jnp.float32)
    mine = jnp.sum(full.reshape(-1, RANK, D + KV) * owned[:, None, None], axis=0)
    return grads[None], mine[None, None, :, :D], mine[None, None, :, D:]


def solution(mesh):
    return jax.shard_map(
        body,
        mesh=mesh,
        in_specs=(
            P("section", "dp", None),
            P("dp", None),
            P("dp"),
            P(),
            P("section", "dp", None),
            P("section", "dp", None),
            P("section", None, None),
        ),
        out_specs=(
            P("section", "dp", None),
            P("section", "dp", None, None),
            P("section", "dp", None, None),
        ),
        check_vma=False,
    )
```

```python
import jax
import jax.numpy as jnp
from jax import lax
from jax.experimental import pallas as pl
from jax.experimental.pallas import tpu as pltpu
from jax.sharding import PartitionSpec as P

MESH = pl.DeviceIdType.MESH
NY, NZ, NX, NC = 4, 8, 4, 2
D = 8192
KV = 512
TR = 128
RANK = 16
WA = KV + TR
WIDE = 1024 + 128
ROWS = 128
SUB = ROWS // NY
COLS = NZ * NX * SUB


def mm(a, b):
    return lax.dot_general(a, b, (((1,), (0,)), ((), ())), preferred_element_type=jnp.float32)


def mm_t(a, b):
    return lax.dot_general(a, b, (((1,), (1,)), ((), ())), preferred_element_type=jnp.float32)


def chain_kernel(
    g0_ref, fz_ref, aa_ref, bb_ref, ids_ref,
    out_ref, vb_ref,
    ob, wab, gall, rbuf, g0v, gsend, pb, rsr, vball, bbuf, perm,
    ring_s, ring_r, y_s, yo_r, yw_r, b_r, g_sem, sib_sem, rs_s, rs_r, vb_s, vb_r, out_s, out_r,
):
    y = lax.axis_index("section")
    d = lax.axis_index("dp")
    z = d // (NX * NC)
    x = (d // NC) % NX
    c = d % NC

    def dev(yy, zz, xx, cc):
        return (yy, zz * (NX * NC) + xx * NC + cc)

    xr, xl = (x + 1) % NX, (x + NX - 1) % NX
    xo = (x + 2) % NX
    zr, zl = (z + 1) % NZ, (z + NZ - 1) % NZ
    sib = 1 - c
    pending = []

    def send(src, dst, ssem, rsem, device):
        copy = pltpu.make_async_remote_copy(
            src_ref=src, dst_ref=dst, send_sem=ssem, recv_sem=rsem,
            device_id=device, device_id_type=MESH,
        )
        copy.start()
        pending.append(copy)

    def landed(dst, rsem):
        pltpu.make_async_copy(dst, dst, rsem).wait()

    load = pltpu.make_async_copy(g0_ref, g0v, g_sem)
    load.start()

    column = [
        (dq, dc, (y + dq) % NY, (c + dc) % NC)
        for dq in range(NY) for dc in range(NC) if dq or dc
    ]
    barrier = pltpu.get_barrier_semaphore()
    for _, _, yy, cc in column:
        pl.semaphore_signal(barrier, inc=1, device_id=dev(yy, z, x, cc), device_id_type=MESH)
    for zz, xx in ((z, xr), (z, xl), (zr, x), (zl, x)):
        pl.semaphore_signal(barrier, inc=1, device_id=dev(y, zz, xx, c), device_id_type=MESH)
    pl.semaphore_wait(barrier, 11)

    local = []
    for dq in range(NY):
        yy = (y + dq) % NY
        rows = pl.ds(pl.multiple_of(yy * SUB, SUB), SUB)
        parts = (
            (fz_ref.at[rows, pl.ds(KV, KV)], ob.at[y, z, x], yo_r.at[y]),
            (fz_ref.at[rows, pl.ds(0, KV)], wab.at[y, z, x, :, pl.ds(0, KV)], yw_r.at[y]),
            (aa_ref.at[rows, :], wab.at[y, z, x, :, pl.ds(KV, TR)], yw_r.at[y]),
            (bb_ref, bbuf.at[y], b_r.at[y]),
        )
        for i, (src, dst, rsem) in enumerate(parts):
            if dq:
                send(src, dst, y_s.at[dq, i], rsem, dev(yy, z, x, c))
            else:
                copy = pltpu.make_async_copy(src, dst, rsem)
                copy.start()

    half = SUB // 2

    def ring(piece, k):
        s = NY - 1 - piece // 2
        is_o = piece % 2 == 0
        buf = ob if is_o else wab
        width = KV if is_o else WA
        lo, hi = pl.ds(0, 256), pl.ds(256, width - 256)
        top, low = pl.ds(0, half), pl.ds(half, half)

        def step(part, stage, moves):
            for way, (src, dst) in enumerate(moves):
                zz, xx = dst
                send(src, src, ring_s.at[piece, part, stage, way],
                     ring_r.at[piece, part, stage, way], dev(y, zz, xx, c))

        def arrive(part, stage, refs):
            for way, ref in enumerate(refs):
                landed(ref, ring_r.at[piece, part, stage, way])

        def zb(by):
            return (z + by + NZ) % NZ

        right, left = (z, xr), (z, xl)
        up, down = (zr, x), (zl, x)
        a_recv = [
            (buf.at[s, z, xl, top], buf.at[s, z, xr, top]),
            (buf.at[s, z, xo, top, lo], buf.at[s, z, xo, top, hi]),
            (buf.at[s, zb(-1), :, top], buf.at[s, zb(1), :, top]),
            (buf.at[s, zb(-2), :, top], buf.at[s, zb(2), :, top]),
            (buf.at[s, zb(-3), :, top], buf.at[s, zb(3), :, top]),
            (buf.at[s, zb(4), pl.ds(0, 2), top], buf.at[s, zb(4), pl.ds(2, 2), top]),
        ]
        a_send = [
            ((buf.at[s, z, x, top], right), (buf.at[s, z, x, top], left)),
            ((buf.at[s, z, xl, top, lo], right), (buf.at[s, z, xr, top, hi], left)),
            ((buf.at[s, z, :, top], up), (buf.at[s, z, :, top], down)),
            ((buf.at[s, zb(-1), :, top], up), (buf.at[s, zb(1), :, top], down)),
            ((buf.at[s, zb(-2), :, top], up), (buf.at[s, zb(2), :, top], down)),
            ((buf.at[s, zb(-3), pl.ds(0, 2), top], up), (buf.at[s, zb(3), pl.ds(2, 2), top], down)),
        ]
        b_recv = [
            (buf.at[s, zb(-1), x, low], buf.at[s, zb(1), x, low]),
            (buf.at[s, zb(-2), x, low], buf.at[s, zb(2), x, low]),
            (buf.at[s, zb(-3), x, low], buf.at[s, zb(3), x, low]),
            (buf.at[s, zb(4), x, low, lo], buf.at[s, zb(4), x, low, hi]),
            (buf.at[s, :, xl, low], buf.at[s, :, xr, low]),
            (buf.at[s, pl.ds(0, 4), xo, low], buf.at[s, pl.ds(4, 4), xo, low]),
        ]
        b_send = [
            ((buf.at[s, z, x, low], up), (buf.at[s, z, x, low], down)),
            ((buf.at[s, zb(-1), x, low], up), (buf.at[s, zb(1), x, low], down)),
            ((buf.at[s, zb(-2), x, low], up), (buf.at[s, zb(2), x, low], down)),
            ((buf.at[s, zb(-3), x, low, lo], up), (buf.at[s, zb(3), x, low, hi], down)),
            ((buf.at[s, :, x, low], right), (buf.at[s, :, x, low], left)),
            ((buf.at[s, pl.ds(0, 4), xl, low], right), (buf.at[s, pl.ds(4, 4), xr, low], left)),
        ]
        if k == 0:
            landed(buf.at[s, z, x], (yo_r if is_o else yw_r).at[s])
        else:
            arrive(0, k - 1, a_recv[k - 1])
            arrive(1, k - 1, b_recv[k - 1])
        if k < 6:
            step(0, k, a_send[k])
            step(1, k, b_send[k])

    def compact():
        load.wait()
        source = lax.broadcasted_iota(jnp.int32, (NX * NC * ROWS, ROWS), 0)
        target = lax.broadcasted_iota(jnp.int32, (NX * NC * ROWS, ROWS), 1)
        base = (target // SUB) * (NC * ROWS) + target % SUB + y * SUB
        mine = (source == base + c * ROWS).astype(jnp.bfloat16)
        other = (source == base + sib * ROWS).astype(jnp.bfloat16)
        own = pl.ds(pl.multiple_of(c * ROWS, ROWS), ROWS)

        for zz in range(NZ):
            block = g0v[:, zz * 1024:(zz + 1) * 1024]
            gsend[:, zz * ROWS:(zz + 1) * ROWS] = mm(block, other).astype(jnp.bfloat16)
        send(gsend, gall.at[NY, own], sib_sem.at[0], sib_sem.at[1], dev(y, z, x, sib))
        for zz in range(NZ):
            block = g0v[:, zz * 1024:(zz + 1) * 1024]
            gall[NY, own, zz * ROWS:(zz + 1) * ROWS] = mm(block, mine).astype(jnp.bfloat16)
        landed(gsend, sib_sem.at[1])

        p_in = lax.broadcasted_iota(jnp.int32, (NY * ROWS, NY * ROWS), 0)
        p_out = lax.broadcasted_iota(jnp.int32, (NY * ROWS, NY * ROWS), 1)
        want = ((p_out // SUB) % NY) * ROWS + (p_out // ROWS) * SUB + p_out % SUB
        perm[...] = (p_in == want).astype(jnp.bfloat16)

    def block_of(yy, cc):
        return pl.ds(pl.multiple_of(cc * ROWS + yy * SUB, SUB), SUB)

    def partial(s):
        right = ob[s].reshape(COLS, KV)
        pb[s] = mm(gall[s + 1], right).astype(jnp.bfloat16)
        for dq, dc, yy, cc in column:
            j = dq * NC + dc
            send(pb.at[s, block_of(yy, cc)], rsr.at[s, j], rs_s.at[s, j], rs_r.at[s, j], dev(yy, z, x, cc))

    def finalise(s):
        total = pb[s, block_of(y, c), :].astype(jnp.float32)
        for dq, dc, _, _ in column:
            j = dq * NC + dc
            landed(rsr.at[s, j], rs_r.at[s, j])
            total = total + rsr[s, j].astype(jnp.float32)
        value = total.astype(jnp.bfloat16)
        landed(bbuf.at[s], b_r.at[s])
        ids = ids_ref[pl.ds(pl.multiple_of(y * SUB, SUB), SUB), :]
        columns = lax.broadcasted_iota(jnp.int32, (SUB, TR), 1) // RANK
        mask = (columns == ids).astype(jnp.float32)
        back = (mask * mm_t(value, bbuf[s])).astype(jnp.bfloat16)
        here = block_of(y, c)
        vball[s, here, 0:KV] = value
        vball[s, here, KV:WA] = (2.0 * back.astype(jnp.float32)).astype(jnp.bfloat16)
        for dq, dc, yy, cc in column:
            j = dq * NC + dc
            send(vball.at[s, here], vball.at[s, here], vb_s.at[s, j], vb_r.at[s, j], dev(yy, z, x, cc))

    def update(s):
        for dq, dc, _, _ in column:
            j = dq * NC + dc
            there = block_of((y - dq + NY) % NY, (c - dc + NC) % NC)
            landed(vball.at[s, there], vb_r.at[s, j])
        for i in range(4):
            cols = slice(i * 256, (i + 1) * 256)
            right = wab[s, 2 * i:2 * i + 2].reshape(256, WA)
            delta = mm_t(vball[s], right)
            gall[s, :, cols] = (gall[s + 1, :, cols].astype(jnp.float32) + delta).astype(jnp.bfloat16)
        own = pl.ds(pl.multiple_of(c * ROWS, ROWS), ROWS)
        others = pl.ds(pl.multiple_of(sib * ROWS, ROWS), ROWS)
        dq = (s - y + NY) % NY
        send(gall.at[s, others], rbuf.at[y, c], out_s.at[s, 1], out_r.at[dq * 2 + 1], dev(s, z, x, sib))
        direct = pltpu.make_async_remote_copy(
            src_ref=gall.at[s, own], dst_ref=rbuf.at[y, c], send_sem=out_s.at[s, 0], recv_sem=out_r.at[dq * 2],
            device_id=dev(s, z, x, c), device_id_type=MESH,
        )
        keep = pltpu.make_async_copy(gall.at[s, own], rbuf.at[y, c], out_r.at[0])

        @pl.when(y != s)
        def _():
            direct.start()

        @pl.when(y == s)
        def _():
            keep.start()

    compact()
    for t in range(15):
        for piece in range(8):
            if 0 <= t - piece <= 6:
                ring(piece, t - piece)
        if t >= 6 and t % 2 == 0:
            i = (t - 6) // 2
            if i > 0:
                update(NY - i)
            if i < NY:
                partial(NY - 1 - i)
        elif t >= 7:
            finalise(NY - 1 - (t - 7) // 2)

    vb_ref[...] = vball[y, pl.ds(pl.multiple_of(c * ROWS, ROWS), ROWS), :]
    for j in range(NY * NC):
        landed(rbuf.at[(y - j // 2 + NY) % NY, (c - j % 2 + NC) % NC], out_r.at[j])
    for zz in range(NZ):
        for cc in range(NC):
            block = jnp.concatenate([rbuf[q, cc, :, zz * ROWS:(zz + 1) * ROWS] for q in range(NY)], axis=1)
            mixed = mm(block, perm[...]).astype(jnp.bfloat16)
            for xx in range(NX):
                at = zz * 1024 + xx * 256 + cc * ROWS
                out_ref[:, at:at + ROWS] = mixed[:, xx * ROWS:(xx + 1) * ROWS]

    for s in range(NY):
        @pl.when(y != s)
        def _(s=s):
            own = pl.ds(pl.multiple_of(c * ROWS, ROWS), ROWS)
            pltpu.make_async_copy(gall.at[s, own], gall.at[s, own], out_s.at[s, 0]).wait()
    for copy in pending:
        copy.wait_send()


def chain(g0, fz, aa, bb, ids):
    vmem = pl.BlockSpec(memory_space=pltpu.VMEM)
    dma = pltpu.SemaphoreType.DMA
    bf = jnp.bfloat16
    return pl.pallas_call(
        chain_kernel,
        out_shape=(
            jax.ShapeDtypeStruct((ROWS, D), bf),
            jax.ShapeDtypeStruct((ROWS, WA), bf),
        ),
        in_specs=[pl.BlockSpec(memory_space=pl.ANY), vmem, vmem, vmem, vmem],
        out_specs=(vmem, vmem),
        scratch_shapes=[
            pltpu.VMEM((NY, NZ, NX, SUB, KV), bf),
            pltpu.VMEM((NY, NZ, NX, SUB, WA), bf),
            pltpu.VMEM((NY + 1, NC * ROWS, COLS), bf),
            pltpu.VMEM((NY, NC, ROWS, COLS), bf),
            pltpu.VMEM((ROWS, D), bf),
            pltpu.VMEM((ROWS, COLS), bf),
            pltpu.VMEM((NY, NC * ROWS, KV), bf),
            pltpu.VMEM((NY, NY * NC, SUB, KV), bf),
            pltpu.VMEM((NY, NC * ROWS, WA), bf),
            pltpu.VMEM((NY, TR, KV), bf),
            pltpu.VMEM((NY * ROWS, NY * ROWS), bf),
            dma((8, 2, 6, 2)),
            dma((8, 2, 6, 2)),
            dma((NY, 4)),
            dma((NY,)),
            dma((NY,)),
            dma((NY,)),
            dma,
            dma((2,)),
            dma((NY, NY * NC)),
            dma((NY, NY * NC)),
            dma((NY, NY * NC)),
            dma((NY, NY * NC)),
            dma((NY, 2)),
            dma((NY * NC,)),
        ],
        compiler_params=pltpu.CompilerParams(
            collective_id=0, has_side_effects=True, vmem_limit_bytes=50 * 2**20
        ),
        cost_estimate=pl.CostEstimate(flops=4 * 10**9, bytes_accessed=10**7, transcendentals=0),
    )(g0, fz, aa, bb, ids)


def reduce_kernel(
    x_ref, vb_ref, low_ref, pick_ref,
    oa_ref, ob_ref,
    xv, gs, gm, gp, hop_l, hop_r, from_l, from_r, hs, js, zr, tall, fs, fin,
    x_sem, p_s, p_r, x_s, x_r, z_s, z_r, t_s, t_r, f_s, f_r,
):
    y = lax.axis_index("section")
    d = lax.axis_index("dp")
    z = d // (NX * NC)
    x = (d // NC) % NX
    c = d % NC
    sib = 1 - c
    bf = jnp.bfloat16

    def dev(zz, xx, cc):
        return (y, zz * (NX * NC) + xx * NC + cc)

    pending = []

    def send(src, dst, ssem, rsem, device):
        copy = pltpu.make_async_remote_copy(
            src_ref=src, dst_ref=dst, send_sem=ssem, recv_sem=rsem,
            device_id=device, device_id_type=MESH,
        )
        copy.start()
        pending.append(copy)

    def landed(dst, rsem):
        pltpu.make_async_copy(dst, dst, rsem).wait()

    load = pltpu.make_async_copy(x_ref, xv, x_sem)
    load.start()
    row = [
        (dx, dc, (x + dx) % NX, (c + dc) % NC)
        for dx in range(NX) for dc in range(NC) if dx or dc
    ]
    barrier = pltpu.get_barrier_semaphore()
    for _, _, xx, cc in row:
        pl.semaphore_signal(barrier, inc=1, device_id=dev(z, xx, cc), device_id_type=MESH)
    for dz in range(1, NZ):
        pl.semaphore_signal(barrier, inc=1, device_id=dev((z + dz) % NZ, x, c), device_id_type=MESH)
    pl.semaphore_wait(barrier, 14)

    eye = (
        lax.broadcasted_iota(jnp.int32, (ROWS, ROWS), 0) == lax.broadcasted_iota(jnp.int32, (ROWS, ROWS), 1)
    ).astype(bf)
    back_t = mm_t(eye, vb_ref[:, KV:WA]).astype(bf)
    low_t = mm_t(eye, low_ref[...]).astype(bf)
    offsets = (2, 1, 3, 0)
    load.wait()

    def term(cc, i, ref):
        xx = (x + offsets[i]) % NX
        cols = pl.ds(pl.multiple_of((cc * NX + xx) * 1024, 1024), 1024)
        ref[i, :, 0:1024] = mm(back_t, xv[:, cols]).astype(bf)
        mine = vb_ref[:, pl.ds(pl.multiple_of(xx * 128, 128), 128)]
        ref[i, :, 1024:WIDE] = (2.0 * mm(low_t, mine)).astype(bf)

    for i in range(NX):
        term(sib, i, gs)
        send(gs.at[i], gp.at[i], p_s.at[i], p_r.at[i], dev(z, x, sib))
    for i in range(NX):
        term(c, i, gm)

    h = ROWS // 2
    top, bot = pl.ds(0, h), pl.ds(h, h)
    xr, xl = (x + 1) % NX, (x + 3) % NX

    def pair(i, rows):
        return gm[i, rows, :].astype(jnp.float32) + gp[i, rows, :].astype(jnp.float32)

    landed(gp.at[0], p_r.at[0])
    hs[0] = pair(0, pl.ds(0, ROWS)).astype(bf)
    send(hs.at[0, top], hop_l, x_s.at[0], x_r.at[0], dev(z, xr, c))
    send(hs.at[0, bot], hop_r, x_s.at[1], x_r.at[1], dev(z, xl, c))
    landed(gp.at[1], p_r.at[1])
    hs[1, bot, :] = pair(1, bot).astype(bf)
    send(hs.at[1, bot], from_l.at[bot], x_s.at[2], x_r.at[2], dev(z, xr, c))
    landed(gp.at[2], p_r.at[2])
    hs[2, top, :] = pair(2, top).astype(bf)
    send(hs.at[2, top], from_r.at[top], x_s.at[3], x_r.at[3], dev(z, xl, c))
    landed(hop_l, x_r.at[0])
    hs[1, top, :] = (pair(1, top) + hop_l[...].astype(jnp.float32)).astype(bf)
    send(hs.at[1, top], from_l.at[top], x_s.at[4], x_r.at[4], dev(z, xr, c))
    landed(hop_r, x_r.at[1])
    hs[2, bot, :] = (pair(2, bot) + hop_r[...].astype(jnp.float32)).astype(bf)
    send(hs.at[2, bot], from_r.at[bot], x_s.at[5], x_r.at[5], dev(z, xl, c))
    landed(gp.at[3], p_r.at[3])
    landed(from_l.at[bot], x_r.at[2])
    landed(from_r.at[top], x_r.at[3])
    landed(from_l.at[top], x_r.at[4])
    landed(from_r.at[bot], x_r.at[5])
    for k in range(NZ):
        rows = pl.ds(k * RANK, RANK)
        total = pair(3, rows) + from_l[rows, :].astype(jnp.float32) + from_r[rows, :].astype(jnp.float32)
        js[k] = total.astype(bf)
    for dz in range(1, NZ):
        to = (z + dz) % NZ
        send(js.at[to], zr.at[dz], z_s.at[dz], z_r.at[dz], dev(to, x, c))
    total = js[z].astype(jnp.float32)
    for dz in range(1, NZ):
        landed(zr.at[dz], z_r.at[dz])
        total = total + zr[dz].astype(jnp.float32)
    tall[z] = total.astype(bf)
    for dz in range(1, NZ):
        to = (z + dz) % NZ
        send(tall.at[z], tall.at[z], t_s.at[dz], t_r.at[dz], dev(to, x, c))
    for dz in range(1, NZ):
        there = (z + NZ - dz) % NZ
        landed(tall.at[there], t_r.at[dz])
    fs[...] = mm(pick_ref[...], tall[...].reshape(TR, WIDE)).astype(bf).reshape(NC * NX, RANK, WIDE)
    me = c * NX + x
    for dx, dc, xx, cc in row:
        j = dx * NC + dc
        send(fs.at[cc * NX + xx], fin.at[me], f_s.at[j], f_r.at[j], dev(z, xx, cc))
    fin[me] = fs[me]
    for dx, dc, _, _ in row:
        j = dx * NC + dc
        there = ((c - dc + NC) % NC) * NX + (x - dx + NX) % NX
        landed(fin.at[there], f_r.at[j])
    for b in range(NC * NX):
        oa_ref[:, b * 1024:(b + 1) * 1024] = fin[b, :, 0:1024].astype(jnp.float32)
    for xx in range(NX):
        ob_ref[:, xx * 128:(xx + 1) * 128] = fin[xx, :, 1024:WIDE].astype(jnp.float32)
    for copy in pending:
        copy.wait_send()


def reduce_to_owners(inputs, vb, low, pick):
    vmem = pl.BlockSpec(memory_space=pltpu.VMEM)
    dma = pltpu.SemaphoreType.DMA
    bf = jnp.bfloat16
    return pl.pallas_call(
        reduce_kernel,
        out_shape=(
            jax.ShapeDtypeStruct((RANK, D), jnp.float32),
            jax.ShapeDtypeStruct((RANK, KV), jnp.float32),
        ),
        in_specs=[pl.BlockSpec(memory_space=pl.ANY), vmem, vmem, vmem],
        out_specs=(vmem, vmem),
        scratch_shapes=[
            pltpu.VMEM((ROWS, D), bf),
            pltpu.VMEM((NX, ROWS, WIDE), bf),
            pltpu.VMEM((NX, ROWS, WIDE), bf),
            pltpu.VMEM((NX, ROWS, WIDE), bf),
            pltpu.VMEM((ROWS // 2, WIDE), bf),
            pltpu.VMEM((ROWS // 2, WIDE), bf),
            pltpu.VMEM((ROWS, WIDE), bf),
            pltpu.VMEM((ROWS, WIDE), bf),
            pltpu.VMEM((NX, ROWS, WIDE), bf),
            pltpu.VMEM((NZ, RANK, WIDE), bf),
            pltpu.VMEM((NZ, RANK, WIDE), bf),
            pltpu.VMEM((NZ, RANK, WIDE), bf),
            pltpu.VMEM((NC * NX, RANK, WIDE), bf),
            pltpu.VMEM((NC * NX, RANK, WIDE), bf),
            dma,
            dma((NX,)),
            dma((NX,)),
            dma((6,)),
            dma((6,)),
            dma((NZ,)),
            dma((NZ,)),
            dma((NZ,)),
            dma((NZ,)),
            dma((NX * NC,)),
            dma((NX * NC,)),
        ],
        compiler_params=pltpu.CompilerParams(
            collective_id=1, has_side_effects=True, vmem_limit_bytes=40 * 2**20
        ),
        cost_estimate=pl.CostEstimate(flops=4 * 10**8, bytes_accessed=4 * 10**6, transcendentals=0),
    )(inputs, vb, low, pick)


def body(layer_inputs, top_grad, tenant_ids, owner_map, frozen, adapt_a, adapt_b):
    my_data = lax.axis_index("dp")
    inputs = layer_inputs[0]
    down = lax.all_gather(adapt_a[0], "dp", axis=0, tiled=True)
    grads, vb = chain(top_grad, frozen[0], adapt_a[0], adapt_b[0], tenant_ids[:, None])
    columns = lax.broadcasted_iota(jnp.int32, (1, TR), 1) // RANK
    mask = (columns == tenant_ids[:, None]).astype(jnp.float32)
    low = (mask * mm(inputs, down)).astype(jnp.bfloat16)
    place = lax.broadcasted_iota(jnp.int32, (TR, TR), 0)
    entry = lax.broadcasted_iota(jnp.int32, (TR, TR), 1)
    block = place // RANK
    target = (my_data // (NX * NC)) * (NX * NC) + (block % NX) * NC + block // NX
    chosen = (jnp.repeat(owner_map, RANK)[None, :] == target) & (place % RANK == entry % RANK)
    owned_a, owned_b = reduce_to_owners(inputs, vb, low, chosen.astype(jnp.bfloat16))
    return grads[None], owned_a[None, None], owned_b[None, None]


def solution(mesh):
    return jax.shard_map(
        body,
        mesh=mesh,
        in_specs=(
            P("section", "dp", None),
            P("dp", None),
            P("dp"),
            P(),
            P("section", "dp", None),
            P("section", "dp", None),
            P("section", None, None),
        ),
        out_specs=(
            P("section", "dp", None),
            P("section", "dp", None, None),
            P("section", "dp", None, None),
        ),
        check_vma=False,
    )
```

```python
import jax
import jax.numpy as jnp
from jax import lax
from jax.experimental import pallas as pl
from jax.experimental.pallas import tpu as pltpu
from jax.sharding import PartitionSpec as P

MESH = pl.DeviceIdType.MESH
NY, NZ, NX, NC = 4, 8, 4, 2
D = 8192
KV = 512
TR = 128
RANK = 16
WA = KV + TR
WIDE = 1024 + 128
STAGES = 5
PIECES = (("O", 3), ("W", 3), ("O", 2), ("W", 2), ("O", 1), ("W", 1), ("O", 0), ("A", 0), ("W", 0))
ROWS = 128
SUB = ROWS // NY
COLS = NZ * NX * SUB


def mm(a, b):
    return lax.dot_general(a, b, (((1,), (0,)), ((), ())), preferred_element_type=jnp.float32)


def mm_t(a, b):
    return lax.dot_general(a, b, (((1,), (1,)), ((), ())), preferred_element_type=jnp.float32)


def fused_kernel(
    g0_ref, x_ref, fz_ref, aa_ref, bb_ref, ids_ref, pick_ref,
    out_ref, oa_ref, ob_ref,
    ob, wab, afull, gall, rbuf, g0v, xv, gsend, pb, rsr, vball, bbuf, perm,
    gs, gm, gp, hop_l, hop_r, from_l, from_r, hs, js, zr, tall, fs, fin,
    ring_s, ring_r, y_s, yo_r, yw_r, b_r, load_sem, sib_sem, rs_s, rs_r, vb_s, vb_r, out_s, out_r, af_sem,
    p_s, p_r, x_s, x_r, z_s, z_r, t_s, t_r, f_s, f_r,
):
    y = lax.axis_index("section")
    d = lax.axis_index("dp")
    z = d // (NX * NC)
    x = (d // NC) % NX
    c = d % NC
    bf = jnp.bfloat16

    def dev(yy, zz, xx, cc):
        return (yy, zz * (NX * NC) + xx * NC + cc)

    xr, xl, xo = (x + 1) % NX, (x + NX - 1) % NX, (x + 2) % NX
    zr_, zl_ = (z + 1) % NZ, (z + NZ - 1) % NZ
    sib = 1 - c
    own = pl.ds(pl.multiple_of(c * ROWS, ROWS), ROWS)
    others = pl.ds(pl.multiple_of(sib * ROWS, ROWS), ROWS)
    pending = []

    def send(src, dst, ssem, rsem, device):
        copy = pltpu.make_async_remote_copy(
            src_ref=src, dst_ref=dst, send_sem=ssem, recv_sem=rsem,
            device_id=device, device_id_type=MESH,
        )
        copy.start()
        pending.append(copy)

    def landed(dst, rsem):
        pltpu.make_async_copy(dst, dst, rsem).wait()

    load = pltpu.make_async_copy(g0_ref, g0v, load_sem.at[0])
    load.start()
    load_x = pltpu.make_async_copy(x_ref, xv, load_sem.at[1])
    load_x.start()

    column = [
        (dq, dc, (y + dq) % NY, (c + dc) % NC)
        for dq in range(NY) for dc in range(NC) if dq or dc
    ]
    row = [
        (dx, dc, (x + dx) % NX, (c + dc) % NC)
        for dx in range(NX) for dc in range(NC) if dx or dc
    ]
    barrier = pltpu.get_barrier_semaphore()
    for _, _, yy, cc in column:
        pl.semaphore_signal(barrier, inc=1, device_id=dev(yy, z, x, cc), device_id_type=MESH)
    for dx, _, xx, cc in row:
        if dx:
            pl.semaphore_signal(barrier, inc=1, device_id=dev(y, z, xx, cc), device_id_type=MESH)
    for dz in range(1, NZ):
        pl.semaphore_signal(barrier, inc=1, device_id=dev(y, (z + dz) % NZ, x, c), device_id_type=MESH)
    pl.semaphore_wait(barrier, 20)

    for dq in range(NY):
        yy = (y + dq) % NY
        rows = pl.ds(pl.multiple_of(yy * SUB, SUB), SUB)
        parts = (
            (fz_ref.at[rows, pl.ds(KV, KV)], ob.at[y, z, x], yo_r.at[y]),
            (fz_ref.at[rows, pl.ds(0, KV)], wab.at[y, z, x, :, pl.ds(0, KV)], yw_r.at[y]),
            (aa_ref.at[rows, :], wab.at[y, z, x, :, pl.ds(KV, TR)], yw_r.at[y]),
            (bb_ref, bbuf.at[y], b_r.at[y]),
        )
        for i, (src, dst, rsem) in enumerate(parts):
            if dq:
                send(src, dst, y_s.at[dq, i], rsem, dev(yy, z, x, c))
            else:
                pltpu.make_async_copy(src, dst, rsem).start()
    pltpu.make_async_copy(aa_ref, afull.at[z, x, c], load_sem.at[2]).start()

    half = SUB // 2

    def ring(piece, k):
        name, s = PIECES[piece]

        def zb(by):
            return (z + by + NZ) % NZ

        if name == "A":
            quarter = ROWS // 4
            top, low = (0, 2 * quarter), (2 * quarter, 2 * quarter)
            low_lo, low_hi = (2 * quarter, quarter), (3 * quarter, quarter)

            def at(zz, xx, rows):
                return afull.at[zz, xx, c, pl.ds(*rows)]

            lo, hi = at(zb(-3), x, low_lo), at(zb(3), x, low_hi)
            far_lo, far_hi = at(zb(4), x, low_lo), at(zb(4), x, low_hi)
        else:
            buf, width = (ob, KV) if name == "O" else (wab, WA)
            top, low = (0, half), (half, half)

            def at(zz, xx, rows):
                return buf.at[s, zz, xx, pl.ds(*rows)]

            def lanes(zz, first, count):
                return buf.at[s, zz, x, pl.ds(*low), pl.ds(first, count)]

            lo, hi = lanes(zb(-3), 0, 256), lanes(zb(3), 256, width - 256)
            far_lo, far_hi = lanes(zb(4), 0, 256), lanes(zb(4), 256, width - 256)

        everything = slice(None)
        first, last = pl.ds(0, 2), pl.ds(2, 2)
        to_x = [(z, xr), (z, xl), (z, xo)]
        up, down = (zr_, x), (zl_, x)
        a_recv = [
            (at(z, xl, top), at(z, xr, top), at(z, xo, top)),
            (at(zb(-1), everything, top), at(zb(1), everything, top)),
            (at(zb(-2), everything, top), at(zb(2), everything, top)),
            (at(zb(-3), everything, top), at(zb(3), everything, top)),
            (at(zb(4), first, top), at(zb(4), last, top)),
        ]
        a_send = [
            [(at(z, x, top), to) for to in to_x],
            [(at(z, everything, top), up), (at(z, everything, top), down)],
            [(at(zb(-1), everything, top), up), (at(zb(1), everything, top), down)],
            [(at(zb(-2), everything, top), up), (at(zb(2), everything, top), down)],
            [(at(zb(-3), first, top), up), (at(zb(3), last, top), down)],
        ]
        b_recv = [
            (at(zb(-1), x, low), at(zb(1), x, low)),
            (at(zb(-2), x, low), at(zb(2), x, low)),
            (at(zb(-3), x, low), at(zb(3), x, low)),
            (far_lo, far_hi),
            (at(everything, xl, low), at(everything, xr, low), at(everything, xo, low)),
        ]
        b_send = [
            [(at(z, x, low), up), (at(z, x, low), down)],
            [(at(zb(-1), x, low), up), (at(zb(1), x, low), down)],
            [(at(zb(-2), x, low), up), (at(zb(2), x, low), down)],
            [(lo, up), (hi, down)],
            [(at(everything, x, low), to) for to in to_x],
        ]
        if k == 0:
            if name == "A":
                landed(afull.at[z, x, c], load_sem.at[2])
            else:
                landed(buf.at[s, z, x], (yo_r if name == "O" else yw_r).at[s])
        else:
            for part, recv in enumerate((a_recv, b_recv)):
                for way, ref in enumerate(recv[k - 1]):
                    landed(ref, ring_r.at[piece, part, k - 1, way])
        if k < STAGES:
            for part, moves in enumerate((a_send, b_send)):
                for way, (src, (zz, xx)) in enumerate(moves[k]):
                    send(src, src, ring_s.at[piece, part, k, way], ring_r.at[piece, part, k, way],
                         dev(y, zz, xx, c))

    def compact():
        load.wait()
        source = lax.broadcasted_iota(jnp.int32, (NX * NC * ROWS, ROWS), 0)
        target = lax.broadcasted_iota(jnp.int32, (NX * NC * ROWS, ROWS), 1)
        base = (target // SUB) * (NC * ROWS) + target % SUB + y * SUB
        mine = (source == base + c * ROWS).astype(jnp.bfloat16)
        other = (source == base + sib * ROWS).astype(jnp.bfloat16)

        for zz in range(NZ):
            block = g0v[:, zz * 1024:(zz + 1) * 1024]
            gsend[:, zz * ROWS:(zz + 1) * ROWS] = mm(block, other).astype(jnp.bfloat16)
        send(gsend, gall.at[NY, own], sib_sem.at[0], sib_sem.at[1], dev(y, z, x, sib))
        for zz in range(NZ):
            block = g0v[:, zz * 1024:(zz + 1) * 1024]
            gall[NY, own, zz * ROWS:(zz + 1) * ROWS] = mm(block, mine).astype(jnp.bfloat16)
        landed(gsend, sib_sem.at[1])

        p_in = lax.broadcasted_iota(jnp.int32, (NY * ROWS, NY * ROWS), 0)
        p_out = lax.broadcasted_iota(jnp.int32, (NY * ROWS, NY * ROWS), 1)
        want = ((p_out // SUB) % NY) * ROWS + (p_out // ROWS) * SUB + p_out % SUB
        perm[...] = (p_in == want).astype(jnp.bfloat16)

    def block_of(yy, cc):
        return pl.ds(pl.multiple_of(cc * ROWS + yy * SUB, SUB), SUB)

    def partial(s):
        right = ob[s].reshape(COLS, KV)
        pb[s] = mm(gall[s + 1], right).astype(jnp.bfloat16)
        for dq, dc, yy, cc in column:
            j = dq * NC + dc
            send(pb.at[s, block_of(yy, cc)], rsr.at[s, j], rs_s.at[s, j], rs_r.at[s, j], dev(yy, z, x, cc))

    def finalise(s):
        total = pb[s, block_of(y, c), :].astype(jnp.float32)
        for dq, dc, _, _ in column:
            j = dq * NC + dc
            landed(rsr.at[s, j], rs_r.at[s, j])
            total = total + rsr[s, j].astype(jnp.float32)
        value = total.astype(jnp.bfloat16)
        landed(bbuf.at[s], b_r.at[s])
        ids = ids_ref[pl.ds(pl.multiple_of(y * SUB, SUB), SUB), :]
        columns = lax.broadcasted_iota(jnp.int32, (SUB, TR), 1) // RANK
        mask = (columns == ids).astype(jnp.float32)
        back = (mask * mm_t(value, bbuf[s])).astype(jnp.bfloat16)
        here = block_of(y, c)
        vball[s, here, 0:KV] = value
        vball[s, here, KV:WA] = (2.0 * back.astype(jnp.float32)).astype(jnp.bfloat16)
        for dq, dc, yy, cc in column:
            j = dq * NC + dc
            send(vball.at[s, here], vball.at[s, here], vb_s.at[s, j], vb_r.at[s, j], dev(yy, z, x, cc))

    def arrive_vb(s):
        for dq, dc, _, _ in column:
            j = dq * NC + dc
            there = block_of((y - dq + NY) % NY, (c - dc + NC) % NC)
            landed(vball.at[s, there], vb_r.at[s, j])

    def update(s):
        if s:
            arrive_vb(s)
        for i in range(4):
            cols = slice(i * 256, (i + 1) * 256)
            right = wab[s, 2 * i:2 * i + 2].reshape(256, WA)
            delta = mm_t(vball[s], right)
            gall[s, :, cols] = (gall[s + 1, :, cols].astype(jnp.float32) + delta).astype(jnp.bfloat16)

    def deliver(s):
        dq = (s - y + NY) % NY
        send(gall.at[s, others], rbuf.at[y, c], out_s.at[s, 1], out_r.at[dq * 2 + 1], dev(s, z, x, sib))
        direct = pltpu.make_async_remote_copy(
            src_ref=gall.at[s, own], dst_ref=rbuf.at[y, c], send_sem=out_s.at[s, 0], recv_sem=out_r.at[dq * 2],
            device_id=dev(s, z, x, c), device_id_type=MESH,
        )
        keep = pltpu.make_async_copy(gall.at[s, own], rbuf.at[y, c], out_r.at[0])

        @pl.when(y != s)
        def _():
            direct.start()

        @pl.when(y == s)
        def _():
            keep.start()

    def low_terms():
        load_x.wait()
        landed(afull.at[:, :, sib], af_sem.at[1])
        columns = lax.broadcasted_iota(jnp.int32, (ROWS, TR), 1) // RANK
        mask = (columns == ids_ref[...]).astype(jnp.float32)
        total = jnp.zeros((ROWS, TR), jnp.float32)
        for k in range(4):
            right = afull[2 * k:2 * k + 2].reshape(2048, TR)
            total = total + mm(xv[:, k * 2048:(k + 1) * 2048], right)
        low = (mask * total).astype(bf)
        return mm_t(eye, low).astype(bf)

    offsets = (2, 1, 3, 0)

    def term(cc, i, ref):
        xx = (x + offsets[i]) % NX
        cols = pl.ds(pl.multiple_of((cc * NX + xx) * 1024, 1024), 1024)
        ref[i, :, 0:1024] = mm(back_t, xv[:, cols]).astype(bf)
        mine = vball[y, own, pl.ds(pl.multiple_of(xx * 128, 128), 128)]
        ref[i, :, 1024:WIDE] = (2.0 * mm(low_t, mine)).astype(bf)

    eye = (
        lax.broadcasted_iota(jnp.int32, (ROWS, ROWS), 0) == lax.broadcasted_iota(jnp.int32, (ROWS, ROWS), 1)
    ).astype(bf)

    compact()
    for t in range(13):
        for piece in range(9):
            k = t - max(0, piece - 1)
            if 0 <= k <= STAGES:
                ring(piece, k)
        if t >= 5 and t % 2 == 1:
            i = (t - 5) // 2
            if i > 0:
                update(NY - i)
            partial(NY - 1 - i)
            if t == 11:
                send(afull.at[:, :, c], afull.at[:, :, c], af_sem.at[0], af_sem.at[1], dev(y, z, x, sib))
        elif t >= 6:
            finalise(NY - 1 - (t - 6) // 2)
    for s in (3, 2, 1):
        deliver(s)
    low_t = low_terms()
    arrive_vb(0)
    back_t = mm_t(eye, vball[y, own, KV:WA]).astype(bf)

    for i in range(NX):
        term(sib, i, gs)
        send(gs.at[i], gp.at[i], p_s.at[i], p_r.at[i], dev(y, z, x, sib))
    for i in range(NX):
        term(c, i, gm)
    update(0)
    deliver(0)

    h = ROWS // 2
    top, bot = pl.ds(0, h), pl.ds(h, h)

    def pair(i, rows):
        return gm[i, rows, :].astype(jnp.float32) + gp[i, rows, :].astype(jnp.float32)

    landed(gp.at[0], p_r.at[0])
    hs[0] = pair(0, pl.ds(0, ROWS)).astype(bf)
    send(hs.at[0, top], hop_l, x_s.at[0], x_r.at[0], dev(y, z, xr, c))
    send(hs.at[0, bot], hop_r, x_s.at[1], x_r.at[1], dev(y, z, xl, c))
    landed(gp.at[1], p_r.at[1])
    hs[1, bot, :] = pair(1, bot).astype(bf)
    send(hs.at[1, bot], from_l.at[bot], x_s.at[2], x_r.at[2], dev(y, z, xr, c))
    landed(gp.at[2], p_r.at[2])
    hs[2, top, :] = pair(2, top).astype(bf)
    send(hs.at[2, top], from_r.at[top], x_s.at[3], x_r.at[3], dev(y, z, xl, c))
    landed(hop_l, x_r.at[0])
    hs[1, top, :] = (pair(1, top) + hop_l[...].astype(jnp.float32)).astype(bf)
    send(hs.at[1, top], from_l.at[top], x_s.at[4], x_r.at[4], dev(y, z, xr, c))
    landed(hop_r, x_r.at[1])
    hs[2, bot, :] = (pair(2, bot) + hop_r[...].astype(jnp.float32)).astype(bf)
    send(hs.at[2, bot], from_r.at[bot], x_s.at[5], x_r.at[5], dev(y, z, xl, c))
    landed(gp.at[3], p_r.at[3])
    landed(from_l.at[bot], x_r.at[2])
    landed(from_r.at[top], x_r.at[3])
    landed(from_l.at[top], x_r.at[4])
    landed(from_r.at[bot], x_r.at[5])
    for k in range(NZ):
        rows = pl.ds(k * RANK, RANK)
        total = pair(3, rows) + from_l[rows, :].astype(jnp.float32) + from_r[rows, :].astype(jnp.float32)
        js[k] = total.astype(bf)
    for dz in range(1, NZ):
        to = (z + dz) % NZ
        send(js.at[to], zr.at[dz], z_s.at[dz], z_r.at[dz], dev(y, to, x, c))
    total = js[z].astype(jnp.float32)
    for dz in range(1, NZ):
        landed(zr.at[dz], z_r.at[dz])
        total = total + zr[dz].astype(jnp.float32)
    tall[z] = total.astype(bf)
    for dz in range(1, NZ):
        to = (z + dz) % NZ
        send(tall.at[z], tall.at[z], t_s.at[dz], t_r.at[dz], dev(y, to, x, c))
    for j in range(NY * NC):
        landed(rbuf.at[(y - j // 2 + NY) % NY, (c - j % 2 + NC) % NC], out_r.at[j])
    for zz in range(NZ):
        for cc in range(NC):
            block = jnp.concatenate([rbuf[q, cc, :, zz * ROWS:(zz + 1) * ROWS] for q in range(NY)], axis=1)
            mixed = mm(block, perm[...]).astype(jnp.bfloat16)
            for xx in range(NX):
                at = zz * 1024 + xx * 256 + cc * ROWS
                out_ref[:, at:at + ROWS] = mixed[:, xx * ROWS:(xx + 1) * ROWS]

    for dz in range(1, NZ):
        there = (z + NZ - dz) % NZ
        landed(tall.at[there], t_r.at[dz])
    fs[...] = mm(pick_ref[...], tall[...].reshape(TR, WIDE)).astype(bf).reshape(NC * NX, RANK, WIDE)
    me = c * NX + x
    for dx, dc, xx, cc in row:
        j = dx * NC + dc
        send(fs.at[cc * NX + xx], fin.at[me], f_s.at[j], f_r.at[j], dev(y, z, xx, cc))
    fin[me] = fs[me]
    for dx, dc, _, _ in row:
        j = dx * NC + dc
        there = ((c - dc + NC) % NC) * NX + (x - dx + NX) % NX
        landed(fin.at[there], f_r.at[j])
    for b in range(NC * NX):
        oa_ref[:, b * 1024:(b + 1) * 1024] = fin[b, :, 0:1024].astype(jnp.float32)
    for xx in range(NX):
        ob_ref[:, xx * 128:(xx + 1) * 128] = fin[xx, :, 1024:WIDE].astype(jnp.float32)
    for s in range(NY):
        @pl.when(y != s)
        def _(s=s):
            pltpu.make_async_copy(gall.at[s, own], gall.at[s, own], out_s.at[s, 0]).wait()
    for copy in pending:
        copy.wait_send()


def fused(g0, inputs, fz, aa, bb, ids, pick):
    vmem = pl.BlockSpec(memory_space=pltpu.VMEM)
    anywhere = pl.BlockSpec(memory_space=pl.ANY)
    dma = pltpu.SemaphoreType.DMA
    bf = jnp.bfloat16
    return pl.pallas_call(
        fused_kernel,
        out_shape=(
            jax.ShapeDtypeStruct((ROWS, D), bf),
            jax.ShapeDtypeStruct((RANK, D), jnp.float32),
            jax.ShapeDtypeStruct((RANK, KV), jnp.float32),
        ),
        in_specs=[anywhere] * 5 + [vmem] * 2,
        out_specs=(vmem, vmem, vmem),
        scratch_shapes=[
            pltpu.VMEM((NY, NZ, NX, SUB, KV), bf),
            pltpu.VMEM((NY, NZ, NX, SUB, WA), bf),
            pltpu.VMEM((NZ, NX, NC, ROWS, TR), bf),
            pltpu.VMEM((NY + 1, NC * ROWS, COLS), bf),
            pltpu.VMEM((NY, NC, ROWS, COLS), bf),
            pltpu.VMEM((ROWS, D), bf),
            pltpu.VMEM((ROWS, D), bf),
            pltpu.VMEM((ROWS, COLS), bf),
            pltpu.VMEM((NY, NC * ROWS, KV), bf),
            pltpu.VMEM((NY, NY * NC, SUB, KV), bf),
            pltpu.VMEM((NY, NC * ROWS, WA), bf),
            pltpu.VMEM((NY, TR, KV), bf),
            pltpu.VMEM((NY * ROWS, NY * ROWS), bf),
            pltpu.VMEM((NX, ROWS, WIDE), bf),
            pltpu.VMEM((NX, ROWS, WIDE), bf),
            pltpu.VMEM((NX, ROWS, WIDE), bf),
            pltpu.VMEM((ROWS // 2, WIDE), bf),
            pltpu.VMEM((ROWS // 2, WIDE), bf),
            pltpu.VMEM((ROWS, WIDE), bf),
            pltpu.VMEM((ROWS, WIDE), bf),
            pltpu.VMEM((NX, ROWS, WIDE), bf),
            pltpu.VMEM((NZ, RANK, WIDE), bf),
            pltpu.VMEM((NZ, RANK, WIDE), bf),
            pltpu.VMEM((NZ, RANK, WIDE), bf),
            pltpu.VMEM((NC * NX, RANK, WIDE), bf),
            pltpu.VMEM((NC * NX, RANK, WIDE), bf),
            dma((9, 2, STAGES, 3)),
            dma((9, 2, STAGES, 3)),
            dma((NY, 4)),
            dma((NY,)),
            dma((NY,)),
            dma((NY,)),
            dma((3,)),
            dma((2,)),
            dma((NY, NY * NC)),
            dma((NY, NY * NC)),
            dma((NY, NY * NC)),
            dma((NY, NY * NC)),
            dma((NY, 2)),
            dma((NY * NC,)),
            dma((2,)),
            dma((NX,)),
            dma((NX,)),
            dma((6,)),
            dma((6,)),
            dma((NZ,)),
            dma((NZ,)),
            dma((NZ,)),
            dma((NZ,)),
            dma((NX * NC,)),
            dma((NX * NC,)),
        ],
        compiler_params=pltpu.CompilerParams(
            collective_id=0, has_side_effects=True, vmem_limit_bytes=56 * 2**20
        ),
        cost_estimate=pl.CostEstimate(flops=5 * 10**9, bytes_accessed=10**7, transcendentals=0),
    )(g0, inputs, fz, aa, bb, ids, pick)


def body(layer_inputs, top_grad, tenant_ids, owner_map, frozen, adapt_a, adapt_b):
    my_data = lax.axis_index("dp")
    place = lax.broadcasted_iota(jnp.int32, (TR, TR), 0)
    entry = lax.broadcasted_iota(jnp.int32, (TR, TR), 1)
    block = place // RANK
    target = (my_data // (NX * NC)) * (NX * NC) + (block % NX) * NC + block // NX
    chosen = (jnp.repeat(owner_map, RANK)[None, :] == target) & (place % RANK == entry % RANK)
    grads, owned_a, owned_b = fused(
        top_grad, layer_inputs[0], frozen[0], adapt_a[0], adapt_b[0],
        tenant_ids[:, None], chosen.astype(jnp.bfloat16),
    )
    return grads[None], owned_a[None, None], owned_b[None, None]


def solution(mesh):
    return jax.shard_map(
        body,
        mesh=mesh,
        in_specs=(
            P("section", "dp", None),
            P("dp", None),
            P("dp"),
            P(),
            P("section", "dp", None),
            P("section", "dp", None),
            P("section", None, None),
        ),
        out_specs=(
            P("section", "dp", None),
            P("section", "dp", None, None),
            P("section", "dp", None, None),
        ),
        check_vma=False,
    )
```

```python
import jax
import jax.numpy as jnp
from jax import lax
from jax.experimental import pallas as pl
from jax.experimental.pallas import tpu as pltpu
from jax.sharding import PartitionSpec as P

MESH = pl.DeviceIdType.MESH
NY, NZ, NX, NC = 4, 8, 4, 2
D = 8192
KV = 512
TR = 128
RANK = 16
WA = KV + TR
WIDE = 1024 + 128
STAGES = 5
PIECES = (("O", 3), ("W", 3), ("O", 2), ("W", 2), ("O", 1), ("W", 1), ("O", 0), ("A", 0), ("W", 0))
DONE = {piece: i for i, piece in enumerate(PIECES)}
ROWS = 128
SUB = ROWS // NY
COLS = NZ * NX * SUB


def mm(a, b):
    return lax.dot_general(a, b, (((1,), (0,)), ((), ())), preferred_element_type=jnp.float32)


def mm_t(a, b):
    return lax.dot_general(a, b, (((1,), (1,)), ((), ())), preferred_element_type=jnp.float32)


def fused_kernel(
    g0_ref, x_ref, fz_ref, aa_ref, bb_ref, ids_ref, owner_ref,
    out_ref, oa_ref, ob_ref,
    ob, wab, afull, gall, rbuf, g0v, xv, gsend, pb, rsr, vball, bbuf, perm, mask, pick, outv,
    gs, gm, gp, hop_l, hop_r, from_l, from_r, hs, js, zr, tall, fs, fin,
    ring_s, ring_r, y_s, yo_r, yw_r, b_r, load_sem, sib_sem, rs_s, rs_r, vb_s, vb_r, out_s, out_r, af_sem,
    p_s, p_r, x_s, x_r, z_s, z_r, t_s, t_r, f_s, f_r, o_sem,
):
    y = lax.axis_index("section")
    d = lax.axis_index("dp")
    z = d // (NX * NC)
    x = (d // NC) % NX
    c = d % NC
    bf = jnp.bfloat16

    def dev(yy, zz, xx, cc):
        return (yy, zz * (NX * NC) + xx * NC + cc)

    xr, xl, xo = (x + 1) % NX, (x + NX - 1) % NX, (x + 2) % NX
    zr_, zl_ = (z + 1) % NZ, (z + NZ - 1) % NZ
    sib = 1 - c
    own = pl.ds(pl.multiple_of(c * ROWS, ROWS), ROWS)
    others = pl.ds(pl.multiple_of(sib * ROWS, ROWS), ROWS)
    pending = []

    def send(src, dst, ssem, rsem, device):
        copy = pltpu.make_async_remote_copy(
            src_ref=src, dst_ref=dst, send_sem=ssem, recv_sem=rsem,
            device_id=device, device_id_type=MESH,
        )
        copy.start()
        pending.append(copy)

    def landed(dst, rsem):
        pltpu.make_async_copy(dst, dst, rsem).wait()

    load = pltpu.make_async_copy(g0_ref, g0v, load_sem.at[0])
    load.start()
    load_x = pltpu.make_async_copy(x_ref, xv, load_sem.at[1])
    load_x.start()

    column = [
        (dq, dc, (y + dq) % NY, (c + dc) % NC)
        for dq in range(NY) for dc in range(NC) if dq or dc
    ]
    row = [
        (dx, dc, (x + dx) % NX, (c + dc) % NC)
        for dx in range(NX) for dc in range(NC) if dx or dc
    ]
    barrier = pltpu.get_barrier_semaphore()
    for _, _, yy, cc in column:
        pl.semaphore_signal(barrier, inc=1, device_id=dev(yy, z, x, cc), device_id_type=MESH)
    for dx, _, xx, cc in row:
        if dx:
            pl.semaphore_signal(barrier, inc=1, device_id=dev(y, z, xx, cc), device_id_type=MESH)
    for dz in range(1, NZ):
        pl.semaphore_signal(barrier, inc=1, device_id=dev(y, (z + dz) % NZ, x, c), device_id_type=MESH)
    pl.semaphore_wait(barrier, 20)

    for dq in range(NY):
        yy = (y + dq) % NY
        rows = pl.ds(pl.multiple_of(yy * SUB, SUB), SUB)
        parts = (
            (fz_ref.at[rows, pl.ds(KV, KV)], ob.at[y, z, x], yo_r.at[y]),
            (fz_ref.at[rows, pl.ds(0, KV)], wab.at[y, z, x, :, pl.ds(0, KV)], yw_r.at[y]),
            (aa_ref.at[rows, :], wab.at[y, z, x, :, pl.ds(KV, TR)], yw_r.at[y]),
        )
        for i, (src, dst, rsem) in enumerate(parts):
            if dq:
                send(src, dst, y_s.at[dq, i], rsem, dev(yy, z, x, c))
            else:
                pltpu.make_async_copy(src, dst, rsem).start()
    pltpu.make_async_copy(aa_ref, afull.at[z, x, c], load_sem.at[2]).start()

    def send_b():
        for dq in range(1, NY):
            send(bb_ref, bbuf.at[y], y_s.at[dq, 3], b_r.at[y], dev((y + dq) % NY, z, x, c))
        pltpu.make_async_copy(bb_ref, bbuf.at[y], b_r.at[y]).start()

    eye = lax.broadcasted_iota(jnp.int32, (ROWS, ROWS), 0) == lax.broadcasted_iota(jnp.int32, (ROWS, ROWS), 1)
    tenant = jnp.sum(eye.astype(jnp.float32) * ids_ref[...].astype(jnp.float32), axis=1, keepdims=True)
    slot = lax.broadcasted_iota(jnp.int32, (ROWS, TR), 1) // RANK
    mask[...] = (slot.astype(jnp.float32) == tenant).astype(jnp.float32)
    eye = eye.astype(bf)
    owner = jnp.zeros((TR, TR), jnp.int32)
    for k in range(TR // RANK):
        owner = owner + (slot == k).astype(jnp.int32) * owner_ref[k]
    place = lax.broadcasted_iota(jnp.int32, (TR, TR), 0)
    entry = lax.broadcasted_iota(jnp.int32, (TR, TR), 1)
    block = place // RANK
    target = z * (NX * NC) + (block % NX) * NC + block // NX
    pick[...] = ((owner == target) & (place % RANK == entry % RANK)).astype(bf)

    half = SUB // 2

    def ring(piece, k):
        name, s = PIECES[piece]

        def zb(by):
            return (z + by + NZ) % NZ

        if name == "A":
            quarter = ROWS // 4
            top, low = (0, 2 * quarter), (2 * quarter, 2 * quarter)
            low_lo, low_hi = (2 * quarter, quarter), (3 * quarter, quarter)

            def at(zz, xx, rows):
                return afull.at[zz, xx, c, pl.ds(*rows)]

            lo, hi = at(zb(-3), x, low_lo), at(zb(3), x, low_hi)
            far_lo, far_hi = at(zb(4), x, low_lo), at(zb(4), x, low_hi)
        else:
            buf, width = (ob, KV) if name == "O" else (wab, WA)
            top, low = (0, half), (half, half)

            def at(zz, xx, rows):
                return buf.at[s, zz, xx, pl.ds(*rows)]

            def lanes(zz, first, count):
                return buf.at[s, zz, x, pl.ds(*low), pl.ds(first, count)]

            lo, hi = lanes(zb(-3), 0, 256), lanes(zb(3), 256, width - 256)
            far_lo, far_hi = lanes(zb(4), 0, 256), lanes(zb(4), 256, width - 256)

        everything = slice(None)
        first, last = pl.ds(0, 2), pl.ds(2, 2)
        to_x = [(z, xr), (z, xl), (z, xo)]
        up, down = (zr_, x), (zl_, x)
        a_recv = [
            (at(z, xl, top), at(z, xr, top), at(z, xo, top)),
            (at(zb(-1), everything, top), at(zb(1), everything, top)),
            (at(zb(-2), everything, top), at(zb(2), everything, top)),
            (at(zb(-3), everything, top), at(zb(3), everything, top)),
            (at(zb(4), first, top), at(zb(4), last, top)),
        ]
        a_send = [
            [(at(z, x, top), to) for to in to_x],
            [(at(z, everything, top), up), (at(z, everything, top), down)],
            [(at(zb(-1), everything, top), up), (at(zb(1), everything, top), down)],
            [(at(zb(-2), everything, top), up), (at(zb(2), everything, top), down)],
            [(at(zb(-3), first, top), up), (at(zb(3), last, top), down)],
        ]
        b_recv = [
            (at(zb(-1), x, low), at(zb(1), x, low)),
            (at(zb(-2), x, low), at(zb(2), x, low)),
            (at(zb(-3), x, low), at(zb(3), x, low)),
            (far_lo, far_hi),
            (at(everything, xl, low), at(everything, xr, low), at(everything, xo, low)),
        ]
        b_send = [
            [(at(z, x, low), up), (at(z, x, low), down)],
            [(at(zb(-1), x, low), up), (at(zb(1), x, low), down)],
            [(at(zb(-2), x, low), up), (at(zb(2), x, low), down)],
            [(lo, up), (hi, down)],
            [(at(everything, x, low), to) for to in to_x],
        ]
        if k == 0:
            if name == "A":
                landed(afull.at[z, x, c], load_sem.at[2])
            else:
                landed(buf.at[s, z, x], (yo_r if name == "O" else yw_r).at[s])
        else:
            for part, recv in enumerate((a_recv, b_recv)):
                for way, ref in enumerate(recv[k - 1]):
                    landed(ref, ring_r.at[piece, part, k - 1, way])
        if k < STAGES:
            for part, moves in enumerate((a_send, b_send)):
                for way, (src, (zz, xx)) in enumerate(moves[k]):
                    send(src, src, ring_s.at[piece, part, k, way], ring_r.at[piece, part, k, way],
                         dev(y, zz, xx, c))

    def compact():
        load.wait()
        source = lax.broadcasted_iota(jnp.int32, (NX * NC * ROWS, ROWS), 0)
        target = lax.broadcasted_iota(jnp.int32, (NX * NC * ROWS, ROWS), 1)
        base = (target // SUB) * (NC * ROWS) + target % SUB + y * SUB
        mine = (source == base + c * ROWS).astype(jnp.bfloat16)
        other = (source == base + sib * ROWS).astype(jnp.bfloat16)

        for zz in range(NZ):
            block = g0v[:, zz * 1024:(zz + 1) * 1024]
            gsend[:, zz * ROWS:(zz + 1) * ROWS] = mm(block, other).astype(jnp.bfloat16)
        send(gsend, gall.at[NY, own], sib_sem.at[0], sib_sem.at[1], dev(y, z, x, sib))
        for zz in range(NZ):
            block = g0v[:, zz * 1024:(zz + 1) * 1024]
            gall[NY, own, zz * ROWS:(zz + 1) * ROWS] = mm(block, mine).astype(jnp.bfloat16)
        landed(gsend, sib_sem.at[1])

        p_in = lax.broadcasted_iota(jnp.int32, (NY * ROWS, NY * ROWS), 0)
        p_out = lax.broadcasted_iota(jnp.int32, (NY * ROWS, NY * ROWS), 1)
        want = ((p_out // SUB) % NY) * ROWS + (p_out // ROWS) * SUB + p_out % SUB
        perm[...] = (p_in == want).astype(jnp.bfloat16)

    def block_of(yy, cc):
        return pl.ds(pl.multiple_of(cc * ROWS + yy * SUB, SUB), SUB)

    def partial(s):
        right = ob[s].reshape(COLS, KV)
        pb[s] = mm(gall[s + 1], right).astype(jnp.bfloat16)
        for dq, dc, yy, cc in column:
            j = dq * NC + dc
            send(pb.at[s, block_of(yy, cc)], rsr.at[s, j], rs_s.at[s, j], rs_r.at[s, j], dev(yy, z, x, cc))

    def finalise(s):
        total = pb[s, block_of(y, c), :].astype(jnp.float32)
        for dq, dc, _, _ in column:
            j = dq * NC + dc
            landed(rsr.at[s, j], rs_r.at[s, j])
            total = total + rsr[s, j].astype(jnp.float32)
        value = total.astype(jnp.bfloat16)
        landed(bbuf.at[s], b_r.at[s])
        here_mask = mask[pl.ds(pl.multiple_of(y * SUB, SUB), SUB), :]
        back = (here_mask * mm_t(value, bbuf[s])).astype(jnp.bfloat16)
        here = block_of(y, c)
        vball[s, here, 0:KV] = value
        vball[s, here, KV:WA] = (2.0 * back.astype(jnp.float32)).astype(jnp.bfloat16)
        for dq, dc, yy, cc in column:
            j = dq * NC + dc
            send(vball.at[s, here], vball.at[s, here], vb_s.at[s, j], vb_r.at[s, j], dev(yy, z, x, cc))

    def arrive_vb(s):
        for dq, dc, _, _ in column:
            j = dq * NC + dc
            there = block_of((y - dq + NY) % NY, (c - dc + NC) % NC)
            landed(vball.at[s, there], vb_r.at[s, j])

    def update(s):
        if s:
            arrive_vb(s)
        for i in range(4):
            cols = slice(i * 256, (i + 1) * 256)
            right = wab[s, 2 * i:2 * i + 2].reshape(256, WA)
            delta = mm_t(vball[s], right)
            gall[s, :, cols] = (gall[s + 1, :, cols].astype(jnp.float32) + delta).astype(jnp.bfloat16)

    def deliver(s):
        dq = (s - y + NY) % NY
        send(gall.at[s, others], rbuf.at[y, c], out_s.at[s, 1], out_r.at[dq * 2 + 1], dev(s, z, x, sib))
        direct = pltpu.make_async_remote_copy(
            src_ref=gall.at[s, own], dst_ref=rbuf.at[y, c], send_sem=out_s.at[s, 0], recv_sem=out_r.at[dq * 2],
            device_id=dev(s, z, x, c), device_id_type=MESH,
        )
        keep = pltpu.make_async_copy(gall.at[s, own], rbuf.at[y, c], out_r.at[0])

        @pl.when(y != s)
        def _():
            direct.start()

        @pl.when(y == s)
        def _():
            keep.start()

    def low_terms():
        load_x.wait()
        landed(afull.at[:, :, sib], af_sem.at[1])
        total = jnp.zeros((ROWS, TR), jnp.float32)
        for k in range(4):
            right = afull[2 * k:2 * k + 2].reshape(2048, TR)
            total = total + mm(xv[:, k * 2048:(k + 1) * 2048], right)
        low = (mask[...] * total).astype(bf)
        return mm_t(eye, low).astype(bf)

    offsets = (2, 1, 3, 0)

    def term(cc, i, ref):
        xx = (x + offsets[i]) % NX
        cols = pl.ds(pl.multiple_of((cc * NX + xx) * 1024, 1024), 1024)
        ref[i, :, 0:1024] = mm(back_t, xv[:, cols]).astype(bf)
        mine = vball[y, own, pl.ds(pl.multiple_of(xx * 128, 128), 128)]
        ref[i, :, 1024:WIDE] = (2.0 * mm(low_t, mine)).astype(bf)

    for t in range(12):
        for piece in range(9):
            k = t - max(0, piece - 1)
            if 0 <= k < STAGES:
                ring(piece, k)
        if t == 0:
            compact()
        if t == 1:
            send_b()
        if t >= 5 and t % 2 == 1:
            i = (t - 5) // 2
            if i > 0:
                ring(DONE["W", NY - i], STAGES)
                update(NY - i)
            ring(DONE["O", NY - 1 - i], STAGES)
            partial(NY - 1 - i)
        elif t >= 6:
            finalise(NY - 1 - (t - 6) // 2)
    ring(DONE["A", 0], STAGES)
    send(afull.at[:, :, c], afull.at[:, :, c], af_sem.at[0], af_sem.at[1], dev(y, z, x, sib))
    finalise(0)
    for s in (3, 2, 1):
        deliver(s)
    low_t = low_terms()
    arrive_vb(0)
    back_t = mm_t(eye, vball[y, own, KV:WA]).astype(bf)

    for i in range(NX):
        term(sib, i, gs)
        send(gs.at[i], gp.at[i], p_s.at[i], p_r.at[i], dev(y, z, x, sib))
    for i in range(NX):
        term(c, i, gm)

    h = ROWS // 2
    top, bot = pl.ds(0, h), pl.ds(h, h)

    def pair(i, rows):
        return gm[i, rows, :].astype(jnp.float32) + gp[i, rows, :].astype(jnp.float32)

    landed(gp.at[0], p_r.at[0])
    hs[0] = pair(0, pl.ds(0, ROWS)).astype(bf)
    send(hs.at[0, top], hop_l, x_s.at[0], x_r.at[0], dev(y, z, xr, c))
    send(hs.at[0, bot], hop_r, x_s.at[1], x_r.at[1], dev(y, z, xl, c))
    landed(gp.at[1], p_r.at[1])
    hs[1, bot, :] = pair(1, bot).astype(bf)
    send(hs.at[1, bot], from_l.at[bot], x_s.at[2], x_r.at[2], dev(y, z, xr, c))
    landed(gp.at[2], p_r.at[2])
    hs[2, top, :] = pair(2, top).astype(bf)
    send(hs.at[2, top], from_r.at[top], x_s.at[3], x_r.at[3], dev(y, z, xl, c))
    ring(DONE["W", 0], STAGES)
    update(0)
    deliver(0)
    landed(hop_l, x_r.at[0])
    hs[1, top, :] = (pair(1, top) + hop_l[...].astype(jnp.float32)).astype(bf)
    send(hs.at[1, top], from_l.at[top], x_s.at[4], x_r.at[4], dev(y, z, xr, c))
    landed(hop_r, x_r.at[1])
    hs[2, bot, :] = (pair(2, bot) + hop_r[...].astype(jnp.float32)).astype(bf)
    send(hs.at[2, bot], from_r.at[bot], x_s.at[5], x_r.at[5], dev(y, z, xl, c))
    landed(gp.at[3], p_r.at[3])
    landed(from_l.at[bot], x_r.at[2])
    landed(from_r.at[top], x_r.at[3])
    landed(from_l.at[top], x_r.at[4])
    landed(from_r.at[bot], x_r.at[5])
    for k in range(NZ):
        rows = pl.ds(k * RANK, RANK)
        total = pair(3, rows) + from_l[rows, :].astype(jnp.float32) + from_r[rows, :].astype(jnp.float32)
        js[k] = total.astype(bf)
    for dz in range(1, NZ):
        to = (z + dz) % NZ
        send(js.at[to], zr.at[dz], z_s.at[dz], z_r.at[dz], dev(y, to, x, c))
    total = js[z].astype(jnp.float32)
    for dz in range(1, NZ):
        landed(zr.at[dz], z_r.at[dz])
        total = total + zr[dz].astype(jnp.float32)
    tall[z] = total.astype(bf)
    for dz in range(1, NZ):
        to = (z + dz) % NZ
        send(tall.at[z], tall.at[z], t_s.at[dz], t_r.at[dz], dev(y, to, x, c))
    for j in range(NY * NC):
        landed(rbuf.at[(y - j // 2 + NY) % NY, (c - j % 2 + NC) % NC], out_r.at[j])
    for zz in range(NZ):
        for cc in range(NC):
            block = jnp.concatenate([rbuf[q, cc, :, zz * ROWS:(zz + 1) * ROWS] for q in range(NY)], axis=1)
            mixed = mm(block, perm[...]).astype(jnp.bfloat16)
            for xx in range(NX):
                at = zz * 1024 + xx * 256 + cc * ROWS
                outv[:, at:at + ROWS] = mixed[:, xx * ROWS:(xx + 1) * ROWS]
        cols = pl.ds(zz * 1024, 1024)
        pltpu.make_async_copy(outv.at[:, cols], out_ref.at[:, cols], o_sem.at[zz]).start()

    for dz in range(1, NZ):
        there = (z + NZ - dz) % NZ
        landed(tall.at[there], t_r.at[dz])
    fs[...] = mm(pick[...], tall[...].reshape(TR, WIDE)).astype(bf).reshape(NC * NX, RANK, WIDE)
    me = c * NX + x
    for dx, dc, xx, cc in row:
        j = dx * NC + dc
        send(fs.at[cc * NX + xx], fin.at[me], f_s.at[j], f_r.at[j], dev(y, z, xx, cc))
    fin[me] = fs[me]
    for dx, dc, _, _ in row:
        j = dx * NC + dc
        there = ((c - dc + NC) % NC) * NX + (x - dx + NX) % NX
        landed(fin.at[there], f_r.at[j])
    for b in range(NC * NX):
        oa_ref[:, b * 1024:(b + 1) * 1024] = fin[b, :, 0:1024].astype(jnp.float32)
    for xx in range(NX):
        ob_ref[:, xx * 128:(xx + 1) * 128] = fin[xx, :, 1024:WIDE].astype(jnp.float32)
    for s in range(NY):
        @pl.when(y != s)
        def _(s=s):
            pltpu.make_async_copy(gall.at[s, own], gall.at[s, own], out_s.at[s, 0]).wait()
    for zz in range(NZ):
        cols = pl.ds(zz * 1024, 1024)
        pltpu.make_async_copy(outv.at[:, cols], out_ref.at[:, cols], o_sem.at[zz]).wait()
    for copy in pending:
        copy.wait_send()


def fused(g0, inputs, fz, aa, bb, ids, owner):
    vmem = pl.BlockSpec(memory_space=pltpu.VMEM)
    anywhere = pl.BlockSpec(memory_space=pl.ANY)
    dma = pltpu.SemaphoreType.DMA
    bf = jnp.bfloat16
    return pl.pallas_call(
        fused_kernel,
        out_shape=(
            jax.ShapeDtypeStruct((ROWS, D), bf),
            jax.ShapeDtypeStruct((RANK, D), jnp.float32),
            jax.ShapeDtypeStruct((RANK, KV), jnp.float32),
        ),
        in_specs=[anywhere] * 5 + [vmem, pl.BlockSpec(memory_space=pltpu.SMEM)],
        out_specs=(anywhere, vmem, vmem),
        scratch_shapes=[
            pltpu.VMEM((NY, NZ, NX, SUB, KV), bf),
            pltpu.VMEM((NY, NZ, NX, SUB, WA), bf),
            pltpu.VMEM((NZ, NX, NC, ROWS, TR), bf),
            pltpu.VMEM((NY + 1, NC * ROWS, COLS), bf),
            pltpu.VMEM((NY, NC, ROWS, COLS), bf),
            pltpu.VMEM((ROWS, D), bf),
            pltpu.VMEM((ROWS, D), bf),
            pltpu.VMEM((ROWS, COLS), bf),
            pltpu.VMEM((NY, NC * ROWS, KV), bf),
            pltpu.VMEM((NY, NY * NC, SUB, KV), bf),
            pltpu.VMEM((NY, NC * ROWS, WA), bf),
            pltpu.VMEM((NY, TR, KV), bf),
            pltpu.VMEM((NY * ROWS, NY * ROWS), bf),
            pltpu.VMEM((ROWS, TR), jnp.float32),
            pltpu.VMEM((TR, TR), bf),
            pltpu.VMEM((ROWS, D), bf),
            pltpu.VMEM((NX, ROWS, WIDE), bf),
            pltpu.VMEM((NX, ROWS, WIDE), bf),
            pltpu.VMEM((NX, ROWS, WIDE), bf),
            pltpu.VMEM((ROWS // 2, WIDE), bf),
            pltpu.VMEM((ROWS // 2, WIDE), bf),
            pltpu.VMEM((ROWS, WIDE), bf),
            pltpu.VMEM((ROWS, WIDE), bf),
            pltpu.VMEM((NX, ROWS, WIDE), bf),
            pltpu.VMEM((NZ, RANK, WIDE), bf),
            pltpu.VMEM((NZ, RANK, WIDE), bf),
            pltpu.VMEM((NZ, RANK, WIDE), bf),
            pltpu.VMEM((NC * NX, RANK, WIDE), bf),
            pltpu.VMEM((NC * NX, RANK, WIDE), bf),
            dma((9, 2, STAGES, 3)),
            dma((9, 2, STAGES, 3)),
            dma((NY, 4)),
            dma((NY,)),
            dma((NY,)),
            dma((NY,)),
            dma((3,)),
            dma((2,)),
            dma((NY, NY * NC)),
            dma((NY, NY * NC)),
            dma((NY, NY * NC)),
            dma((NY, NY * NC)),
            dma((NY, 2)),
            dma((NY * NC,)),
            dma((2,)),
            dma((NX,)),
            dma((NX,)),
            dma((6,)),
            dma((6,)),
            dma((NZ,)),
            dma((NZ,)),
            dma((NZ,)),
            dma((NZ,)),
            dma((NX * NC,)),
            dma((NX * NC,)),
            dma((NZ,)),
        ],
        compiler_params=pltpu.CompilerParams(
            collective_id=0, has_side_effects=True, vmem_limit_bytes=56 * 2**20
        ),
        cost_estimate=pl.CostEstimate(flops=5 * 10**9, bytes_accessed=10**7, transcendentals=0),
    )(g0, inputs, fz, aa, bb, ids, owner)


def body(layer_inputs, top_grad, tenant_ids, owner_map, frozen, adapt_a, adapt_b):
    grads, owned_a, owned_b = fused(
        top_grad, layer_inputs[0], frozen[0], adapt_a[0], adapt_b[0], tenant_ids[None, :], owner_map
    )
    return grads[None], owned_a[None, None], owned_b[None, None]


def solution(mesh):
    return jax.shard_map(
        body,
        mesh=mesh,
        in_specs=(
            P("section", "dp", None),
            P("dp", None),
            P("dp"),
            P(),
            P("section", "dp", None),
            P("section", "dp", None),
            P("section", None, None),
        ),
        out_specs=(
            P("section", "dp", None),
            P("section", "dp", None, None),
            P("section", "dp", None, None),
        ),
        check_vma=False,
    )
```

```python
import jax
import jax.numpy as jnp
from jax import lax
from jax.experimental import pallas as pl
from jax.experimental.pallas import tpu as pltpu
from jax.sharding import PartitionSpec as P

MESH = pl.DeviceIdType.MESH
NY, NZ, NX, NC = 4, 8, 4, 2
D = 8192
KV = 512
TR = 128
RANK = 16
WA = KV + TR
WIDE = 1024 + 128
STAGES = 5
PIECES = (("O", 3), ("W", 3), ("O", 2), ("W", 2), ("O", 1), ("W", 1), ("O", 0), ("A", 0), ("W", 0))
DONE = {piece: i for i, piece in enumerate(PIECES)}
ROWS = 128
SUB = ROWS // NY
COLS = NZ * NX * SUB


def mm(a, b):
    return lax.dot_general(a, b, (((1,), (0,)), ((), ())), preferred_element_type=jnp.float32)


def mm_t(a, b):
    return lax.dot_general(a, b, (((1,), (1,)), ((), ())), preferred_element_type=jnp.float32)


def fused_kernel(
    g0_ref, x_ref, fz_ref, aa_ref, bb_ref, ids_ref, owner_ref,
    out_ref, oa_ref, ob_ref,
    ob, wab, afull, gall, rbuf, g0v, xv, gsend, pb, rsr, vball, bbuf, perm, mask, pick, outv,
    gs, gm, gp, hop_l, hop_r, from_l, from_r, hs, js, zr, tall, fs, fin,
    ring_s, ring_r, y_s, yo_r, yw_r, b_r, load_sem, sib_sem, rs_s, rs_r, vb_s, vb_r, out_s, out_r, af_sem,
    p_s, p_r, x_s, x_r, z_s, z_r, t_s, t_r, f_s, f_r, o_sem,
):
    y = lax.axis_index("section")
    d = lax.axis_index("dp")
    z = d // (NX * NC)
    x = (d // NC) % NX
    c = d % NC
    bf = jnp.bfloat16

    def dev(yy, zz, xx, cc):
        return (yy, zz * (NX * NC) + xx * NC + cc)

    xr, xl, xo = (x + 1) % NX, (x + NX - 1) % NX, (x + 2) % NX
    zr_, zl_ = (z + 1) % NZ, (z + NZ - 1) % NZ
    sib = 1 - c
    own = pl.ds(pl.multiple_of(c * ROWS, ROWS), ROWS)
    others = pl.ds(pl.multiple_of(sib * ROWS, ROWS), ROWS)
    pending = []

    def send(src, dst, ssem, rsem, device):
        copy = pltpu.make_async_remote_copy(
            src_ref=src, dst_ref=dst, send_sem=ssem, recv_sem=rsem,
            device_id=device, device_id_type=MESH,
        )
        copy.start()
        pending.append(copy)

    def landed(dst, rsem):
        pltpu.make_async_copy(dst, dst, rsem).wait()

    load = pltpu.make_async_copy(g0_ref, g0v, load_sem.at[0])
    load.start()
    load_x = pltpu.make_async_copy(x_ref, xv, load_sem.at[1])
    load_x.start()

    column = [
        (dq, dc, (y + dq) % NY, (c + dc) % NC)
        for dq in range(NY) for dc in range(NC) if dq or dc
    ]
    row = [
        (dx, dc, (x + dx) % NX, (c + dc) % NC)
        for dx in range(NX) for dc in range(NC) if dx or dc
    ]
    barrier = pltpu.get_barrier_semaphore()
    for _, _, yy, cc in column:
        pl.semaphore_signal(barrier, inc=1, device_id=dev(yy, z, x, cc), device_id_type=MESH)
    for dx, _, xx, cc in row:
        if dx:
            pl.semaphore_signal(barrier, inc=1, device_id=dev(y, z, xx, cc), device_id_type=MESH)
    for dz in range(1, NZ):
        pl.semaphore_signal(barrier, inc=1, device_id=dev(y, (z + dz) % NZ, x, c), device_id_type=MESH)
    pl.semaphore_wait(barrier, 20)

    for dq in range(NY):
        yy = (y + dq) % NY
        rows = pl.ds(pl.multiple_of(yy * SUB, SUB), SUB)
        parts = (
            (fz_ref.at[rows, pl.ds(KV, KV)], ob.at[y, z, x], yo_r.at[y]),
            (fz_ref.at[rows, pl.ds(0, KV)], wab.at[y, z, x, :, pl.ds(0, KV)], yw_r.at[y]),
            (aa_ref.at[rows, :], wab.at[y, z, x, :, pl.ds(KV, TR)], yw_r.at[y]),
        )
        for i, (src, dst, rsem) in enumerate(parts):
            if dq:
                send(src, dst, y_s.at[dq, i], rsem, dev(yy, z, x, c))
            else:
                pltpu.make_async_copy(src, dst, rsem).start()
    pltpu.make_async_copy(aa_ref, afull.at[z, x, c], load_sem.at[2]).start()

    def send_b():
        for dq in range(1, NY):
            send(bb_ref, bbuf.at[y], y_s.at[dq, 3], b_r.at[y], dev((y + dq) % NY, z, x, c))
        pltpu.make_async_copy(bb_ref, bbuf.at[y], b_r.at[y]).start()

    eye = lax.broadcasted_iota(jnp.int32, (ROWS, ROWS), 0) == lax.broadcasted_iota(jnp.int32, (ROWS, ROWS), 1)
    tenant = jnp.sum(eye.astype(jnp.float32) * ids_ref[...].astype(jnp.float32), axis=1, keepdims=True)
    slot = lax.broadcasted_iota(jnp.int32, (ROWS, TR), 1) // RANK
    mask[...] = (slot.astype(jnp.float32) == tenant).astype(jnp.float32)
    eye = eye.astype(bf)
    owner = jnp.zeros((TR, TR), jnp.int32)
    for k in range(TR // RANK):
        owner = owner + (slot == k).astype(jnp.int32) * owner_ref[k]
    place = lax.broadcasted_iota(jnp.int32, (TR, TR), 0)
    entry = lax.broadcasted_iota(jnp.int32, (TR, TR), 1)
    block = place // RANK
    target = z * (NX * NC) + (block % NX) * NC + block // NX
    pick[...] = ((owner == target) & (place % RANK == entry % RANK)).astype(bf)

    half = SUB // 2

    def ring(piece, k):
        name, s = PIECES[piece]

        def zb(by):
            return (z + by + NZ) % NZ

        if name == "A":
            quarter = ROWS // 4
            top, low = (0, 2 * quarter), (2 * quarter, 2 * quarter)
            low_lo, low_hi = (2 * quarter, quarter), (3 * quarter, quarter)

            def at(zz, xx, rows):
                return afull.at[zz, xx, c, pl.ds(*rows)]

            lo, hi = at(zb(-3), x, low_lo), at(zb(3), x, low_hi)
            far_lo, far_hi = at(zb(4), x, low_lo), at(zb(4), x, low_hi)
        else:
            buf, width = (ob, KV) if name == "O" else (wab, WA)
            top, low = (0, half), (half, half)

            def at(zz, xx, rows):
                return buf.at[s, zz, xx, pl.ds(*rows)]

            def lanes(zz, first, count):
                return buf.at[s, zz, x, pl.ds(*low), pl.ds(first, count)]

            lo, hi = lanes(zb(-3), 0, 256), lanes(zb(3), 256, width - 256)
            far_lo, far_hi = lanes(zb(4), 0, 256), lanes(zb(4), 256, width - 256)

        everything = slice(None)
        first, last = pl.ds(0, 2), pl.ds(2, 2)
        to_x = [(z, xr), (z, xl), (z, xo)]
        up, down = (zr_, x), (zl_, x)
        a_recv = [
            (at(z, xl, top), at(z, xr, top), at(z, xo, top)),
            (at(zb(-1), everything, top), at(zb(1), everything, top)),
            (at(zb(-2), everything, top), at(zb(2), everything, top)),
            (at(zb(-3), everything, top), at(zb(3), everything, top)),
            (at(zb(4), first, top), at(zb(4), last, top)),
        ]
        a_send = [
            [(at(z, x, top), to) for to in to_x],
            [(at(z, everything, top), up), (at(z, everything, top), down)],
            [(at(zb(-1), everything, top), up), (at(zb(1), everything, top), down)],
            [(at(zb(-2), everything, top), up), (at(zb(2), everything, top), down)],
            [(at(zb(-3), first, top), up), (at(zb(3), last, top), down)],
        ]
        b_recv = [
            (at(zb(-1), x, low), at(zb(1), x, low)),
            (at(zb(-2), x, low), at(zb(2), x, low)),
            (at(zb(-3), x, low), at(zb(3), x, low)),
            (far_lo, far_hi),
            (at(everything, xl, low), at(everything, xr, low), at(everything, xo, low)),
        ]
        b_send = [
            [(at(z, x, low), up), (at(z, x, low), down)],
            [(at(zb(-1), x, low), up), (at(zb(1), x, low), down)],
            [(at(zb(-2), x, low), up), (at(zb(2), x, low), down)],
            [(lo, up), (hi, down)],
            [(at(everything, x, low), to) for to in to_x],
        ]
        if k == 0:
            if name == "A":
                landed(afull.at[z, x, c], load_sem.at[2])
            else:
                landed(buf.at[s, z, x], (yo_r if name == "O" else yw_r).at[s])
        else:
            for part, recv in enumerate((a_recv, b_recv)):
                for way, ref in enumerate(recv[k - 1]):
                    landed(ref, ring_r.at[piece, part, k - 1, way])
        if k < STAGES:
            for part, moves in enumerate((a_send, b_send)):
                for way, (src, (zz, xx)) in enumerate(moves[k]):
                    send(src, src, ring_s.at[piece, part, k, way], ring_r.at[piece, part, k, way],
                         dev(y, zz, xx, c))

    def compact():
        load.wait()
        source = lax.broadcasted_iota(jnp.int32, (NX * NC * ROWS, ROWS), 0)
        target = lax.broadcasted_iota(jnp.int32, (NX * NC * ROWS, ROWS), 1)
        base = (target // SUB) * (NC * ROWS) + target % SUB + y * SUB
        mine = (source == base + c * ROWS).astype(jnp.bfloat16)
        other = (source == base + sib * ROWS).astype(jnp.bfloat16)

        for zz in range(NZ):
            block = g0v[:, zz * 1024:(zz + 1) * 1024]
            gsend[:, zz * ROWS:(zz + 1) * ROWS] = mm(block, other).astype(jnp.bfloat16)
        send(gsend, gall.at[NY, own], sib_sem.at[0], sib_sem.at[1], dev(y, z, x, sib))
        for zz in range(NZ):
            block = g0v[:, zz * 1024:(zz + 1) * 1024]
            gall[NY, own, zz * ROWS:(zz + 1) * ROWS] = mm(block, mine).astype(jnp.bfloat16)
        landed(gsend, sib_sem.at[1])

        p_in = lax.broadcasted_iota(jnp.int32, (NY * ROWS, NY * ROWS), 0)
        p_out = lax.broadcasted_iota(jnp.int32, (NY * ROWS, NY * ROWS), 1)
        want = ((p_out // SUB) % NY) * ROWS + (p_out // ROWS) * SUB + p_out % SUB
        perm[...] = (p_in == want).astype(jnp.bfloat16)

    def block_of(yy, cc):
        return pl.ds(pl.multiple_of(cc * ROWS + yy * SUB, SUB), SUB)

    def partial(s):
        right = ob[s].reshape(COLS, KV)
        pb[s] = mm(gall[s + 1], right).astype(jnp.bfloat16)
        for dq, dc, yy, cc in column:
            j = dq * NC + dc
            send(pb.at[s, block_of(yy, cc)], rsr.at[s, j], rs_s.at[s, j], rs_r.at[s, j], dev(yy, z, x, cc))

    def finalise(s):
        total = pb[s, block_of(y, c), :].astype(jnp.float32)
        for dq, dc, _, _ in column:
            j = dq * NC + dc
            landed(rsr.at[s, j], rs_r.at[s, j])
            total = total + rsr[s, j].astype(jnp.float32)
        value = total.astype(jnp.bfloat16)
        landed(bbuf.at[s], b_r.at[s])
        here_mask = mask[pl.ds(pl.multiple_of(y * SUB, SUB), SUB), :]
        back = (here_mask * mm_t(value, bbuf[s])).astype(jnp.bfloat16)
        here = block_of(y, c)
        vball[s, here, 0:KV] = value
        vball[s, here, KV:WA] = (2.0 * back.astype(jnp.float32)).astype(jnp.bfloat16)
        for dq, dc, yy, cc in column:
            j = dq * NC + dc
            send(vball.at[s, here], vball.at[s, here], vb_s.at[s, j], vb_r.at[s, j], dev(yy, z, x, cc))

    def arrive_vb(s):
        for dq, dc, _, _ in column:
            j = dq * NC + dc
            there = block_of((y - dq + NY) % NY, (c - dc + NC) % NC)
            landed(vball.at[s, there], vb_r.at[s, j])

    def update(s):
        if s:
            arrive_vb(s)
        for i in range(4):
            cols = slice(i * 256, (i + 1) * 256)
            right = wab[s, 2 * i:2 * i + 2].reshape(256, WA)
            delta = mm_t(vball[s], right)
            gall[s, :, cols] = (gall[s + 1, :, cols].astype(jnp.float32) + delta).astype(jnp.bfloat16)

    def deliver(s):
        dq = (s - y + NY) % NY
        send(gall.at[s, others], rbuf.at[y, c], out_s.at[s, 1], out_r.at[dq * 2 + 1], dev(s, z, x, sib))
        direct = pltpu.make_async_remote_copy(
            src_ref=gall.at[s, own], dst_ref=rbuf.at[y, c], send_sem=out_s.at[s, 0], recv_sem=out_r.at[dq * 2],
            device_id=dev(s, z, x, c), device_id_type=MESH,
        )
        keep = pltpu.make_async_copy(gall.at[s, own], rbuf.at[y, c], out_r.at[0])

        @pl.when(y != s)
        def _():
            direct.start()

        @pl.when(y == s)
        def _():
            keep.start()

    def low_terms():
        load_x.wait()
        landed(afull.at[:, :, sib], af_sem.at[1])
        total = jnp.zeros((ROWS, TR), jnp.float32)
        for k in range(4):
            right = afull[2 * k:2 * k + 2].reshape(2048, TR)
            total = total + mm(xv[:, k * 2048:(k + 1) * 2048], right)
        low = (mask[...] * total).astype(bf)
        return mm_t(eye, low).astype(bf)

    offsets = (2, 1, 3, 0)

    def term(cc, i, ref):
        xx = (x + offsets[i]) % NX
        cols = pl.ds(pl.multiple_of((cc * NX + xx) * 1024, 1024), 1024)
        ref[i, :, 0:1024] = mm(back_t, xv[:, cols]).astype(bf)
        mine = vball[y, own, pl.ds(pl.multiple_of(xx * 128, 128), 128)]
        ref[i, :, 1024:WIDE] = (2.0 * mm(low_t, mine)).astype(bf)

    for t in range(12):
        for piece in range(9):
            k = t - max(0, piece - 1)
            if 0 <= k < STAGES:
                ring(piece, k)
        if t == 0:
            compact()
        if t == 1:
            send_b()
        if t >= 5 and t % 2 == 1:
            i = (t - 5) // 2
            if i > 0:
                ring(DONE["W", NY - i], STAGES)
                update(NY - i)
            ring(DONE["O", NY - 1 - i], STAGES)
            partial(NY - 1 - i)
        elif t >= 6:
            finalise(NY - 1 - (t - 6) // 2)
    ring(DONE["A", 0], STAGES)
    send(afull.at[:, :, c], afull.at[:, :, c], af_sem.at[0], af_sem.at[1], dev(y, z, x, sib))
    finalise(0)
    for s in (3, 2, 1):
        deliver(s)
    low_t = low_terms()
    arrive_vb(0)
    back_t = mm_t(eye, vball[y, own, KV:WA]).astype(bf)

    for i in range(NX):
        term(sib, i, gs)
        send(gs.at[i], gp.at[i], p_s.at[i], p_r.at[i], dev(y, z, x, sib))
    for i in range(NX):
        term(c, i, gm)

    h = ROWS // 2
    top, bot = pl.ds(0, h), pl.ds(h, h)
    parts = (pl.ds(0, 640), pl.ds(640, 512))

    def pair(i, rows, cut):
        return gm[i, rows, cut].astype(jnp.float32) + gp[i, rows, cut].astype(jnp.float32)

    landed(gp.at[0], p_r.at[0])
    for n, cut in enumerate(parts):
        hs[0, :, cut] = pair(0, pl.ds(0, ROWS), cut).astype(bf)
        send(hs.at[0, top, cut], hop_l.at[:, cut], x_s.at[n, 0], x_r.at[n, 0], dev(y, z, xr, c))
        send(hs.at[0, bot, cut], hop_r.at[:, cut], x_s.at[n, 1], x_r.at[n, 1], dev(y, z, xl, c))
    landed(gp.at[1], p_r.at[1])
    landed(gp.at[2], p_r.at[2])
    for n, cut in enumerate(parts):
        hs[1, bot, cut] = pair(1, bot, cut).astype(bf)
        send(hs.at[1, bot, cut], from_l.at[bot, cut], x_s.at[n, 2], x_r.at[n, 2], dev(y, z, xr, c))
        hs[2, top, cut] = pair(2, top, cut).astype(bf)
        send(hs.at[2, top, cut], from_r.at[top, cut], x_s.at[n, 3], x_r.at[n, 3], dev(y, z, xl, c))
    ring(DONE["W", 0], STAGES)
    update(0)
    deliver(0)
    for n, cut in enumerate(parts):
        landed(hop_l.at[:, cut], x_r.at[n, 0])
        hs[1, top, cut] = (pair(1, top, cut) + hop_l[:, cut].astype(jnp.float32)).astype(bf)
        send(hs.at[1, top, cut], from_l.at[top, cut], x_s.at[n, 4], x_r.at[n, 4], dev(y, z, xr, c))
        landed(hop_r.at[:, cut], x_r.at[n, 1])
        hs[2, bot, cut] = (pair(2, bot, cut) + hop_r[:, cut].astype(jnp.float32)).astype(bf)
        send(hs.at[2, bot, cut], from_r.at[bot, cut], x_s.at[n, 5], x_r.at[n, 5], dev(y, z, xl, c))
    landed(gp.at[3], p_r.at[3])
    for n, cut in enumerate(parts):
        landed(from_l.at[bot, cut], x_r.at[n, 2])
        landed(from_r.at[top, cut], x_r.at[n, 3])
        landed(from_l.at[top, cut], x_r.at[n, 4])
        landed(from_r.at[bot, cut], x_r.at[n, 5])
        for k in range(NZ):
            rows = pl.ds(k * RANK, RANK)
            total = pair(3, rows, cut) + from_l[rows, cut].astype(jnp.float32) + from_r[rows, cut].astype(jnp.float32)
            js[k, :, cut] = total.astype(bf)
        for dz in range(1, NZ):
            to = (z + dz) % NZ
            send(js.at[to, :, cut], zr.at[dz, :, cut], z_s.at[n, dz], z_r.at[n, dz], dev(y, to, x, c))
    for n, cut in enumerate(parts):
        total = js[z, :, cut].astype(jnp.float32)
        for dz in range(1, NZ):
            landed(zr.at[dz, :, cut], z_r.at[n, dz])
            total = total + zr[dz, :, cut].astype(jnp.float32)
        tall[z, :, cut] = total.astype(bf)
        for dz in range(1, NZ):
            to = (z + dz) % NZ
            send(tall.at[z, :, cut], tall.at[z, :, cut], t_s.at[n, dz], t_r.at[n, dz], dev(y, to, x, c))
    me = c * NX + x
    for n, cut in enumerate(parts):
        for dz in range(1, NZ):
            there = (z + NZ - dz) % NZ
            landed(tall.at[there, :, cut], t_r.at[n, dz])
        gathered = tall[:, :, cut].reshape(TR, cut.size)
        fs[:, :, cut] = mm(pick[...], gathered).astype(bf).reshape(NC * NX, RANK, cut.size)
        for dx, dc, xx, cc in row:
            j = dx * NC + dc
            send(fs.at[cc * NX + xx, :, cut], fin.at[me, :, cut], f_s.at[n, j], f_r.at[n, j], dev(y, z, xx, cc))
    fin[me] = fs[me]
    for j in range(NY * NC):
        landed(rbuf.at[(y - j // 2 + NY) % NY, (c - j % 2 + NC) % NC], out_r.at[j])
    for zz in range(NZ):
        for cc in range(NC):
            block = jnp.concatenate([rbuf[q, cc, :, zz * ROWS:(zz + 1) * ROWS] for q in range(NY)], axis=1)
            mixed = mm(block, perm[...]).astype(jnp.bfloat16)
            for xx in range(NX):
                at = zz * 1024 + xx * 256 + cc * ROWS
                outv[:, at:at + ROWS] = mixed[:, xx * ROWS:(xx + 1) * ROWS]
        cols = pl.ds(zz * 1024, 1024)
        pltpu.make_async_copy(outv.at[:, cols], out_ref.at[:, cols], o_sem.at[zz]).start()

    for n, cut in enumerate(parts):
        for dx, dc, _, _ in row:
            j = dx * NC + dc
            there = ((c - dc + NC) % NC) * NX + (x - dx + NX) % NX
            landed(fin.at[there, :, cut], f_r.at[n, j])
    for b in range(NC * NX):
        oa_ref[:, b * 1024:(b + 1) * 1024] = fin[b, :, 0:1024].astype(jnp.float32)
    for xx in range(NX):
        ob_ref[:, xx * 128:(xx + 1) * 128] = fin[xx, :, 1024:WIDE].astype(jnp.float32)
    for s in range(NY):
        @pl.when(y != s)
        def _(s=s):
            pltpu.make_async_copy(gall.at[s, own], gall.at[s, own], out_s.at[s, 0]).wait()
    for zz in range(NZ):
        cols = pl.ds(zz * 1024, 1024)
        pltpu.make_async_copy(outv.at[:, cols], out_ref.at[:, cols], o_sem.at[zz]).wait()
    for copy in pending:
        copy.wait_send()


def fused(g0, inputs, fz, aa, bb, ids, owner):
    vmem = pl.BlockSpec(memory_space=pltpu.VMEM)
    anywhere = pl.BlockSpec(memory_space=pl.ANY)
    dma = pltpu.SemaphoreType.DMA
    bf = jnp.bfloat16
    return pl.pallas_call(
        fused_kernel,
        out_shape=(
            jax.ShapeDtypeStruct((ROWS, D), bf),
            jax.ShapeDtypeStruct((RANK, D), jnp.float32),
            jax.ShapeDtypeStruct((RANK, KV), jnp.float32),
        ),
        in_specs=[anywhere] * 5 + [vmem, pl.BlockSpec(memory_space=pltpu.SMEM)],
        out_specs=(anywhere, vmem, vmem),
        scratch_shapes=[
            pltpu.VMEM((NY, NZ, NX, SUB, KV), bf),
            pltpu.VMEM((NY, NZ, NX, SUB, WA), bf),
            pltpu.VMEM((NZ, NX, NC, ROWS, TR), bf),
            pltpu.VMEM((NY + 1, NC * ROWS, COLS), bf),
            pltpu.VMEM((NY, NC, ROWS, COLS), bf),
            pltpu.VMEM((ROWS, D), bf),
            pltpu.VMEM((ROWS, D), bf),
            pltpu.VMEM((ROWS, COLS), bf),
            pltpu.VMEM((NY, NC * ROWS, KV), bf),
            pltpu.VMEM((NY, NY * NC, SUB, KV), bf),
            pltpu.VMEM((NY, NC * ROWS, WA), bf),
            pltpu.VMEM((NY, TR, KV), bf),
            pltpu.VMEM((NY * ROWS, NY * ROWS), bf),
            pltpu.VMEM((ROWS, TR), jnp.float32),
            pltpu.VMEM((TR, TR), bf),
            pltpu.VMEM((ROWS, D), bf),
            pltpu.VMEM((NX, ROWS, WIDE), bf),
            pltpu.VMEM((NX, ROWS, WIDE), bf),
            pltpu.VMEM((NX, ROWS, WIDE), bf),
            pltpu.VMEM((ROWS // 2, WIDE), bf),
            pltpu.VMEM((ROWS // 2, WIDE), bf),
            pltpu.VMEM((ROWS, WIDE), bf),
            pltpu.VMEM((ROWS, WIDE), bf),
            pltpu.VMEM((NX, ROWS, WIDE), bf),
            pltpu.VMEM((NZ, RANK, WIDE), bf),
            pltpu.VMEM((NZ, RANK, WIDE), bf),
            pltpu.VMEM((NZ, RANK, WIDE), bf),
            pltpu.VMEM((NC * NX, RANK, WIDE), bf),
            pltpu.VMEM((NC * NX, RANK, WIDE), bf),
            dma((9, 2, STAGES, 3)),
            dma((9, 2, STAGES, 3)),
            dma((NY, 4)),
            dma((NY,)),
            dma((NY,)),
            dma((NY,)),
            dma((3,)),
            dma((2,)),
            dma((NY, NY * NC)),
            dma((NY, NY * NC)),
            dma((NY, NY * NC)),
            dma((NY, NY * NC)),
            dma((NY, 2)),
            dma((NY * NC,)),
            dma((2,)),
            dma((NX,)),
            dma((NX,)),
            dma((2, 6)),
            dma((2, 6)),
            dma((2, NZ)),
            dma((2, NZ)),
            dma((2, NZ)),
            dma((2, NZ)),
            dma((2, NX * NC)),
            dma((2, NX * NC)),
            dma((NZ,)),
        ],
        compiler_params=pltpu.CompilerParams(
            collective_id=0, has_side_effects=True, vmem_limit_bytes=56 * 2**20
        ),
        cost_estimate=pl.CostEstimate(flops=5 * 10**9, bytes_accessed=10**7, transcendentals=0),
    )(g0, inputs, fz, aa, bb, ids, owner)


def body(layer_inputs, top_grad, tenant_ids, owner_map, frozen, adapt_a, adapt_b):
    grads, owned_a, owned_b = fused(
        top_grad, layer_inputs[0], frozen[0], adapt_a[0], adapt_b[0], tenant_ids[None, :], owner_map
    )
    return grads[None], owned_a[None, None], owned_b[None, None]


def solution(mesh):
    return jax.shard_map(
        body,
        mesh=mesh,
        in_specs=(
            P("section", "dp", None),
            P("dp", None),
            P("dp"),
            P(),
            P("section", "dp", None),
            P("section", "dp", None),
            P("section", None, None),
        ),
        out_specs=(
            P("section", "dp", None),
            P("section", "dp", None, None),
            P("section", "dp", None, None),
        ),
        check_vma=False,
    )
```

```python
import jax
import jax.numpy as jnp
from jax import lax
from jax.experimental import pallas as pl
from jax.experimental.pallas import tpu as pltpu
from jax.sharding import PartitionSpec as P

MESH = pl.DeviceIdType.MESH
NY, NZ, NX, NC = 4, 8, 4, 2
D = 8192
KV = 512
TR = 128
RANK = 16
WA = KV + TR
WIDE = 1024 + 128
STAGES = 5
PIECES = (("O", 3), ("W", 3), ("O", 2), ("W", 2), ("O", 1), ("W", 1), ("O", 0), ("A", 0), ("W", 0))
DONE = {piece: i for i, piece in enumerate(PIECES)}
ROWS = 128
SUB = ROWS // NY
COLS = NZ * NX * SUB


def mm(a, b):
    return lax.dot_general(a, b, (((1,), (0,)), ((), ())), preferred_element_type=jnp.float32)


def mm_t(a, b):
    return lax.dot_general(a, b, (((1,), (1,)), ((), ())), preferred_element_type=jnp.float32)


def fused_kernel(
    g0_ref, x_ref, fz_ref, aa_ref, bb_ref, ids_ref, owner_ref,
    out_ref, oa_ref, ob_ref,
    ob, wab, afull, gall, rbuf, g0v, xv, gsend, pb, rsr, vball, bbuf, perm, mask, pick, outv,
    gs, gm, gp, hop_l, hop_r, from_l, from_r, hs, js, zr, tall, fs, fin,
    ring_s, ring_r, y_s, yo_r, yw_r, b_r, load_sem, sib_sem, rs_s, rs_r, vb_s, vb_r, out_s, out_r, af_sem,
    p_s, p_r, x_s, x_r, z_s, z_r, t_s, t_r, f_s, f_r, o_sem,
):
    y = lax.axis_index("section")
    d = lax.axis_index("dp")
    z = d // (NX * NC)
    x = (d // NC) % NX
    c = d % NC
    bf = jnp.bfloat16

    def dev(yy, zz, xx, cc):
        return (yy, zz * (NX * NC) + xx * NC + cc)

    xr, xl, xo = (x + 1) % NX, (x + NX - 1) % NX, (x + 2) % NX
    zr_, zl_ = (z + 1) % NZ, (z + NZ - 1) % NZ
    sib = 1 - c
    own = pl.ds(pl.multiple_of(c * ROWS, ROWS), ROWS)
    others = pl.ds(pl.multiple_of(sib * ROWS, ROWS), ROWS)
    pending = []

    def send(src, dst, ssem, rsem, device):
        copy = pltpu.make_async_remote_copy(
            src_ref=src, dst_ref=dst, send_sem=ssem, recv_sem=rsem,
            device_id=device, device_id_type=MESH,
        )
        copy.start()
        pending.append(copy)

    def landed(dst, rsem):
        pltpu.make_async_copy(dst, dst, rsem).wait()

    load = pltpu.make_async_copy(g0_ref, g0v, load_sem.at[0])
    load.start()
    load_x = pltpu.make_async_copy(x_ref, xv, load_sem.at[1])
    load_x.start()

    column = [
        (dq, dc, (y + dq) % NY, (c + dc) % NC)
        for dq in range(NY) for dc in range(NC) if dq or dc
    ]
    row = [
        (dx, dc, (x + dx) % NX, (c + dc) % NC)
        for dx in range(NX) for dc in range(NC) if dx or dc
    ]
    barrier = pltpu.get_barrier_semaphore()
    for _, _, yy, cc in column:
        pl.semaphore_signal(barrier, inc=1, device_id=dev(yy, z, x, cc), device_id_type=MESH)
    for dx, _, xx, cc in row:
        if dx:
            pl.semaphore_signal(barrier, inc=1, device_id=dev(y, z, xx, cc), device_id_type=MESH)
    for dz in range(1, NZ):
        pl.semaphore_signal(barrier, inc=1, device_id=dev(y, (z + dz) % NZ, x, c), device_id_type=MESH)
    pl.semaphore_wait(barrier, 20)

    for i in range(3):
        for dq in range(NY):
            yy = (y + dq) % NY
            rows = pl.ds(pl.multiple_of(yy * SUB, SUB), SUB)
            src, dst, rsem = (
                (fz_ref.at[rows, pl.ds(KV, KV)], ob.at[y, z, x], yo_r.at[y]),
                (fz_ref.at[rows, pl.ds(0, KV)], wab.at[y, z, x, :, pl.ds(0, KV)], yw_r.at[y]),
                (aa_ref.at[rows, :], wab.at[y, z, x, :, pl.ds(KV, TR)], yw_r.at[y]),
            )[i]
            if dq:
                send(src, dst, y_s.at[dq, i], rsem, dev(yy, z, x, c))
            else:
                pltpu.make_async_copy(src, dst, rsem).start()
    pltpu.make_async_copy(aa_ref, afull.at[z, x, c], load_sem.at[2]).start()

    def send_b():
        for dq in range(1, NY):
            send(bb_ref, bbuf.at[y], y_s.at[dq, 3], b_r.at[y], dev((y + dq) % NY, z, x, c))
        pltpu.make_async_copy(bb_ref, bbuf.at[y], b_r.at[y]).start()

    eye = lax.broadcasted_iota(jnp.int32, (ROWS, ROWS), 0) == lax.broadcasted_iota(jnp.int32, (ROWS, ROWS), 1)
    tenant = jnp.sum(eye.astype(jnp.float32) * ids_ref[...].astype(jnp.float32), axis=1, keepdims=True)
    slot = lax.broadcasted_iota(jnp.int32, (ROWS, TR), 1) // RANK
    mask[...] = (slot.astype(jnp.float32) == tenant).astype(jnp.float32)
    eye = eye.astype(bf)
    owner = jnp.zeros((TR, TR), jnp.int32)
    for k in range(TR // RANK):
        owner = owner + (slot == k).astype(jnp.int32) * owner_ref[k]
    place = lax.broadcasted_iota(jnp.int32, (TR, TR), 0)
    entry = lax.broadcasted_iota(jnp.int32, (TR, TR), 1)
    block = place // RANK
    target = z * (NX * NC) + (block % NX) * NC + block // NX
    pick[...] = ((owner == target) & (place % RANK == entry % RANK)).astype(bf)

    half = SUB // 2

    def ring(piece, k):
        name, s = PIECES[piece]

        def zb(by):
            return (z + by + NZ) % NZ

        if name == "A":
            quarter = ROWS // 4
            top, low = (0, 2 * quarter), (2 * quarter, 2 * quarter)
            low_lo, low_hi = (2 * quarter, quarter), (3 * quarter, quarter)

            def at(zz, xx, rows):
                return afull.at[zz, xx, c, pl.ds(*rows)]

            lo, hi = at(zb(-3), x, low_lo), at(zb(3), x, low_hi)
            far_lo, far_hi = at(zb(4), x, low_lo), at(zb(4), x, low_hi)
        else:
            buf, width = (ob, KV) if name == "O" else (wab, WA)
            top, low = (0, half), (half, half)

            def at(zz, xx, rows):
                return buf.at[s, zz, xx, pl.ds(*rows)]

            def lanes(zz, first, count):
                return buf.at[s, zz, x, pl.ds(*low), pl.ds(first, count)]

            lo, hi = lanes(zb(-3), 0, 256), lanes(zb(3), 256, width - 256)
            far_lo, far_hi = lanes(zb(4), 0, 256), lanes(zb(4), 256, width - 256)

        everything = slice(None)
        first, last = pl.ds(0, 2), pl.ds(2, 2)
        to_x = [(z, xr), (z, xl), (z, xo)]
        up, down = (zr_, x), (zl_, x)
        a_recv = [
            (at(z, xl, top), at(z, xr, top), at(z, xo, top)),
            (at(zb(-1), everything, top), at(zb(1), everything, top)),
            (at(zb(-2), everything, top), at(zb(2), everything, top)),
            (at(zb(-3), everything, top), at(zb(3), everything, top)),
            (at(zb(4), first, top), at(zb(4), last, top)),
        ]
        a_send = [
            [(at(z, x, top), to) for to in to_x],
            [(at(z, everything, top), up), (at(z, everything, top), down)],
            [(at(zb(-1), everything, top), up), (at(zb(1), everything, top), down)],
            [(at(zb(-2), everything, top), up), (at(zb(2), everything, top), down)],
            [(at(zb(-3), first, top), up), (at(zb(3), last, top), down)],
        ]
        b_recv = [
            (at(zb(-1), x, low), at(zb(1), x, low)),
            (at(zb(-2), x, low), at(zb(2), x, low)),
            (at(zb(-3), x, low), at(zb(3), x, low)),
            (far_lo, far_hi),
            (at(everything, xl, low), at(everything, xr, low), at(everything, xo, low)),
        ]
        b_send = [
            [(at(z, x, low), up), (at(z, x, low), down)],
            [(at(zb(-1), x, low), up), (at(zb(1), x, low), down)],
            [(at(zb(-2), x, low), up), (at(zb(2), x, low), down)],
            [(lo, up), (hi, down)],
            [(at(everything, x, low), to) for to in to_x],
        ]
        if k == 0:
            if name == "A":
                landed(afull.at[z, x, c], load_sem.at[2])
            else:
                landed(buf.at[s, z, x], (yo_r if name == "O" else yw_r).at[s])
        else:
            for part, recv in enumerate((a_recv, b_recv)):
                for way, ref in enumerate(recv[k - 1]):
                    landed(ref, ring_r.at[piece, part, k - 1, way])
        if k < STAGES:
            for part, moves in enumerate((a_send, b_send)):
                for way, (src, (zz, xx)) in enumerate(moves[k]):
                    send(src, src, ring_s.at[piece, part, k, way], ring_r.at[piece, part, k, way],
                         dev(y, zz, xx, c))

    def compact():
        load.wait()
        source = lax.broadcasted_iota(jnp.int32, (NX * NC * ROWS, ROWS), 0)
        target = lax.broadcasted_iota(jnp.int32, (NX * NC * ROWS, ROWS), 1)
        base = (target // SUB) * (NC * ROWS) + target % SUB + y * SUB
        mine = (source == base + c * ROWS).astype(jnp.bfloat16)
        other = (source == base + sib * ROWS).astype(jnp.bfloat16)

        for zz in range(NZ):
            block = g0v[:, zz * 1024:(zz + 1) * 1024]
            gsend[:, zz * ROWS:(zz + 1) * ROWS] = mm(block, other).astype(jnp.bfloat16)
        send(gsend, gall.at[NY, own], sib_sem.at[0], sib_sem.at[1], dev(y, z, x, sib))
        for zz in range(NZ):
            block = g0v[:, zz * 1024:(zz + 1) * 1024]
            gall[NY, own, zz * ROWS:(zz + 1) * ROWS] = mm(block, mine).astype(jnp.bfloat16)
        landed(gsend, sib_sem.at[1])

        p_in = lax.broadcasted_iota(jnp.int32, (NY * ROWS, NY * ROWS), 0)
        p_out = lax.broadcasted_iota(jnp.int32, (NY * ROWS, NY * ROWS), 1)
        want = ((p_out // SUB) % NY) * ROWS + (p_out // ROWS) * SUB + p_out % SUB
        perm[...] = (p_in == want).astype(jnp.bfloat16)

    def block_of(yy, cc):
        return pl.ds(pl.multiple_of(cc * ROWS + yy * SUB, SUB), SUB)

    def partial(s):
        right = ob[s].reshape(COLS, KV)
        pb[s] = mm(gall[s + 1], right).astype(jnp.bfloat16)
        for dq, dc, yy, cc in column:
            j = dq * NC + dc
            send(pb.at[s, block_of(yy, cc)], rsr.at[s, j], rs_s.at[s, j], rs_r.at[s, j], dev(yy, z, x, cc))

    def finalise(s):
        total = pb[s, block_of(y, c), :].astype(jnp.float32)
        for dq, dc, _, _ in column:
            j = dq * NC + dc
            landed(rsr.at[s, j], rs_r.at[s, j])
            total = total + rsr[s, j].astype(jnp.float32)
        value = total.astype(jnp.bfloat16)
        landed(bbuf.at[s], b_r.at[s])
        here_mask = mask[pl.ds(pl.multiple_of(y * SUB, SUB), SUB), :]
        back = (here_mask * mm_t(value, bbuf[s])).astype(jnp.bfloat16)
        here = block_of(y, c)
        vball[s, here, 0:KV] = value
        vball[s, here, KV:WA] = (2.0 * back.astype(jnp.float32)).astype(jnp.bfloat16)
        for dq, dc, yy, cc in column:
            j = dq * NC + dc
            send(vball.at[s, here], vball.at[s, here], vb_s.at[s, j], vb_r.at[s, j], dev(yy, z, x, cc))

    def arrive_vb(s):
        for dq, dc, _, _ in column:
            j = dq * NC + dc
            there = block_of((y - dq + NY) % NY, (c - dc + NC) % NC)
            landed(vball.at[s, there], vb_r.at[s, j])

    def update(s):
        if s:
            arrive_vb(s)
        for i in range(4):
            cols = slice(i * 256, (i + 1) * 256)
            right = wab[s, 2 * i:2 * i + 2].reshape(256, WA)
            delta = mm_t(vball[s], right)
            gall[s, :, cols] = (gall[s + 1, :, cols].astype(jnp.float32) + delta).astype(jnp.bfloat16)

    def deliver(s):
        dq = (s - y + NY) % NY
        send(gall.at[s, others], rbuf.at[y, c], out_s.at[s, 1], out_r.at[dq * 2 + 1], dev(s, z, x, sib))
        direct = pltpu.make_async_remote_copy(
            src_ref=gall.at[s, own], dst_ref=rbuf.at[y, c], send_sem=out_s.at[s, 0], recv_sem=out_r.at[dq * 2],
            device_id=dev(s, z, x, c), device_id_type=MESH,
        )
        keep = pltpu.make_async_copy(gall.at[s, own], rbuf.at[y, c], out_r.at[0])

        @pl.when(y != s)
        def _():
            direct.start()

        @pl.when(y == s)
        def _():
            keep.start()

    def low_terms():
        load_x.wait()
        landed(afull.at[:, :, sib], af_sem.at[1])
        total = jnp.zeros((ROWS, TR), jnp.float32)
        for k in range(4):
            right = afull[2 * k:2 * k + 2].reshape(2048, TR)
            total = total + mm(xv[:, k * 2048:(k + 1) * 2048], right)
        low = (mask[...] * total).astype(bf)
        return mm_t(eye, low).astype(bf)

    offsets = (2, 1, 3, 0)

    def term(cc, i, ref):
        xx = (x + offsets[i]) % NX
        cols = pl.ds(pl.multiple_of((cc * NX + xx) * 1024, 1024), 1024)
        ref[i, :, 0:1024] = mm(back_t, xv[:, cols]).astype(bf)
        mine = vball[y, own, pl.ds(pl.multiple_of(xx * 128, 128), 128)]
        ref[i, :, 1024:WIDE] = (2.0 * mm(low_t, mine)).astype(bf)

    for t in range(12):
        for piece in range(9):
            k = t - max(0, piece - 1)
            if 0 <= k < STAGES:
                ring(piece, k)
        if t == 0:
            compact()
        if t == 1:
            send_b()
        if t >= 5 and t % 2 == 1:
            i = (t - 5) // 2
            if i > 0:
                ring(DONE["W", NY - i], STAGES)
                update(NY - i)
            ring(DONE["O", NY - 1 - i], STAGES)
            partial(NY - 1 - i)
        elif t >= 6:
            finalise(NY - 1 - (t - 6) // 2)
    ring(DONE["A", 0], STAGES)
    send(afull.at[:, :, c], afull.at[:, :, c], af_sem.at[0], af_sem.at[1], dev(y, z, x, sib))
    finalise(0)
    for s in (3, 2, 1):
        deliver(s)
    low_t = low_terms()
    arrive_vb(0)
    back_t = mm_t(eye, vball[y, own, KV:WA]).astype(bf)

    for i in range(NX):
        term(sib, i, gs)
        send(gs.at[i], gp.at[i], p_s.at[i], p_r.at[i], dev(y, z, x, sib))
    for i in range(NX):
        term(c, i, gm)

    h = ROWS // 2
    top, bot = pl.ds(0, h), pl.ds(h, h)
    parts = (pl.ds(0, 640), pl.ds(640, 512))

    def pair(i, rows, cut):
        return gm[i, rows, cut].astype(jnp.float32) + gp[i, rows, cut].astype(jnp.float32)

    landed(gp.at[0], p_r.at[0])
    for n, cut in enumerate(parts):
        hs[0, :, cut] = pair(0, pl.ds(0, ROWS), cut).astype(bf)
        send(hs.at[0, top, cut], hop_l.at[:, cut], x_s.at[n, 0], x_r.at[n, 0], dev(y, z, xr, c))
        send(hs.at[0, bot, cut], hop_r.at[:, cut], x_s.at[n, 1], x_r.at[n, 1], dev(y, z, xl, c))
    landed(gp.at[1], p_r.at[1])
    landed(gp.at[2], p_r.at[2])
    for n, cut in enumerate(parts):
        hs[1, bot, cut] = pair(1, bot, cut).astype(bf)
        send(hs.at[1, bot, cut], from_l.at[bot, cut], x_s.at[n, 2], x_r.at[n, 2], dev(y, z, xr, c))
        hs[2, top, cut] = pair(2, top, cut).astype(bf)
        send(hs.at[2, top, cut], from_r.at[top, cut], x_s.at[n, 3], x_r.at[n, 3], dev(y, z, xl, c))
    ring(DONE["W", 0], STAGES)
    update(0)
    deliver(0)
    for n, cut in enumerate(parts):
        landed(hop_l.at[:, cut], x_r.at[n, 0])
        hs[1, top, cut] = (pair(1, top, cut) + hop_l[:, cut].astype(jnp.float32)).astype(bf)
        send(hs.at[1, top, cut], from_l.at[top, cut], x_s.at[n, 4], x_r.at[n, 4], dev(y, z, xr, c))
        landed(hop_r.at[:, cut], x_r.at[n, 1])
        hs[2, bot, cut] = (pair(2, bot, cut) + hop_r[:, cut].astype(jnp.float32)).astype(bf)
        send(hs.at[2, bot, cut], from_r.at[bot, cut], x_s.at[n, 5], x_r.at[n, 5], dev(y, z, xl, c))
    landed(gp.at[3], p_r.at[3])
    for n, cut in enumerate(parts):
        landed(from_l.at[bot, cut], x_r.at[n, 2])
        landed(from_r.at[top, cut], x_r.at[n, 3])
        landed(from_l.at[top, cut], x_r.at[n, 4])
        landed(from_r.at[bot, cut], x_r.at[n, 5])
        for k in range(NZ):
            rows = pl.ds(k * RANK, RANK)
            total = pair(3, rows, cut) + from_l[rows, cut].astype(jnp.float32) + from_r[rows, cut].astype(jnp.float32)
            js[k, :, cut] = total.astype(bf)
        for dz in range(1, NZ):
            to = (z + dz) % NZ
            send(js.at[to, :, cut], zr.at[dz, :, cut], z_s.at[n, dz], z_r.at[n, dz], dev(y, to, x, c))
    for n, cut in enumerate(parts):
        total = js[z, :, cut].astype(jnp.float32)
        for dz in range(1, NZ):
            landed(zr.at[dz, :, cut], z_r.at[n, dz])
            total = total + zr[dz, :, cut].astype(jnp.float32)
        tall[z, :, cut] = total.astype(bf)
        for dz in range(1, NZ):
            to = (z + dz) % NZ
            send(tall.at[z, :, cut], tall.at[z, :, cut], t_s.at[n, dz], t_r.at[n, dz], dev(y, to, x, c))
    me = c * NX + x
    for n, cut in enumerate(parts):
        for dz in range(1, NZ):
            there = (z + NZ - dz) % NZ
            landed(tall.at[there, :, cut], t_r.at[n, dz])
        gathered = tall[:, :, cut].reshape(TR, cut.size)
        fs[:, :, cut] = mm(pick[...], gathered).astype(bf).reshape(NC * NX, RANK, cut.size)
        for dx, dc, xx, cc in row:
            j = dx * NC + dc
            send(fs.at[cc * NX + xx, :, cut], fin.at[me, :, cut], f_s.at[n, j], f_r.at[n, j], dev(y, z, xx, cc))
    fin[me] = fs[me]
    for j in range(NY * NC):
        landed(rbuf.at[(y - j // 2 + NY) % NY, (c - j % 2 + NC) % NC], out_r.at[j])
    for zz in range(NZ):
        for cc in range(NC):
            block = jnp.concatenate([rbuf[q, cc, :, zz * ROWS:(zz + 1) * ROWS] for q in range(NY)], axis=1)
            mixed = mm(block, perm[...]).astype(jnp.bfloat16)
            for xx in range(NX):
                at = zz * 1024 + xx * 256 + cc * ROWS
                outv[:, at:at + ROWS] = mixed[:, xx * ROWS:(xx + 1) * ROWS]
        cols = pl.ds(zz * 1024, 1024)
        pltpu.make_async_copy(outv.at[:, cols], out_ref.at[:, cols], o_sem.at[zz]).start()

    for n, cut in enumerate(parts):
        for dx, dc, _, _ in row:
            j = dx * NC + dc
            there = ((c - dc + NC) % NC) * NX + (x - dx + NX) % NX
            landed(fin.at[there, :, cut], f_r.at[n, j])
    for b in range(NC * NX):
        oa_ref[:, b * 1024:(b + 1) * 1024] = fin[b, :, 0:1024].astype(jnp.float32)
    for xx in range(NX):
        ob_ref[:, xx * 128:(xx + 1) * 128] = fin[xx, :, 1024:WIDE].astype(jnp.float32)
    for s in range(NY):
        @pl.when(y != s)
        def _(s=s):
            pltpu.make_async_copy(gall.at[s, own], gall.at[s, own], out_s.at[s, 0]).wait()
    for zz in range(NZ):
        cols = pl.ds(zz * 1024, 1024)
        pltpu.make_async_copy(outv.at[:, cols], out_ref.at[:, cols], o_sem.at[zz]).wait()
    for copy in pending:
        copy.wait_send()


def fused(g0, inputs, fz, aa, bb, ids, owner):
    vmem = pl.BlockSpec(memory_space=pltpu.VMEM)
    anywhere = pl.BlockSpec(memory_space=pl.ANY)
    dma = pltpu.SemaphoreType.DMA
    bf = jnp.bfloat16
    return pl.pallas_call(
        fused_kernel,
        out_shape=(
            jax.ShapeDtypeStruct((ROWS, D), bf),
            jax.ShapeDtypeStruct((RANK, D), jnp.float32),
            jax.ShapeDtypeStruct((RANK, KV), jnp.float32),
        ),
        in_specs=[anywhere] * 5 + [vmem, pl.BlockSpec(memory_space=pltpu.SMEM)],
        out_specs=(anywhere, vmem, vmem),
        scratch_shapes=[
            pltpu.VMEM((NY, NZ, NX, SUB, KV), bf),
            pltpu.VMEM((NY, NZ, NX, SUB, WA), bf),
            pltpu.VMEM((NZ, NX, NC, ROWS, TR), bf),
            pltpu.VMEM((NY + 1, NC * ROWS, COLS), bf),
            pltpu.VMEM((NY, NC, ROWS, COLS), bf),
            pltpu.VMEM((ROWS, D), bf),
            pltpu.VMEM((ROWS, D), bf),
            pltpu.VMEM((ROWS, COLS), bf),
            pltpu.VMEM((NY, NC * ROWS, KV), bf),
            pltpu.VMEM((NY, NY * NC, SUB, KV), bf),
            pltpu.VMEM((NY, NC * ROWS, WA), bf),
            pltpu.VMEM((NY, TR, KV), bf),
            pltpu.VMEM((NY * ROWS, NY * ROWS), bf),
            pltpu.VMEM((ROWS, TR), jnp.float32),
            pltpu.VMEM((TR, TR), bf),
            pltpu.VMEM((ROWS, D), bf),
            pltpu.VMEM((NX, ROWS, WIDE), bf),
            pltpu.VMEM((NX, ROWS, WIDE), bf),
            pltpu.VMEM((NX, ROWS, WIDE), bf),
            pltpu.VMEM((ROWS // 2, WIDE), bf),
            pltpu.VMEM((ROWS // 2, WIDE), bf),
            pltpu.VMEM((ROWS, WIDE), bf),
            pltpu.VMEM((ROWS, WIDE), bf),
            pltpu.VMEM((NX, ROWS, WIDE), bf),
            pltpu.VMEM((NZ, RANK, WIDE), bf),
            pltpu.VMEM((NZ, RANK, WIDE), bf),
            pltpu.VMEM((NZ, RANK, WIDE), bf),
            pltpu.VMEM((NC * NX, RANK, WIDE), bf),
            pltpu.VMEM((NC * NX, RANK, WIDE), bf),
            dma((9, 2, STAGES, 3)),
            dma((9, 2, STAGES, 3)),
            dma((NY, 4)),
            dma((NY,)),
            dma((NY,)),
            dma((NY,)),
            dma((3,)),
            dma((2,)),
            dma((NY, NY * NC)),
            dma((NY, NY * NC)),
            dma((NY, NY * NC)),
            dma((NY, NY * NC)),
            dma((NY, 2)),
            dma((NY * NC,)),
            dma((2,)),
            dma((NX,)),
            dma((NX,)),
            dma((2, 6)),
            dma((2, 6)),
            dma((2, NZ)),
            dma((2, NZ)),
            dma((2, NZ)),
            dma((2, NZ)),
            dma((2, NX * NC)),
            dma((2, NX * NC)),
            dma((NZ,)),
        ],
        compiler_params=pltpu.CompilerParams(
            collective_id=0, has_side_effects=True, vmem_limit_bytes=56 * 2**20
        ),
        cost_estimate=pl.CostEstimate(flops=5 * 10**9, bytes_accessed=10**7, transcendentals=0),
    )(g0, inputs, fz, aa, bb, ids, owner)


def body(layer_inputs, top_grad, tenant_ids, owner_map, frozen, adapt_a, adapt_b):
    grads, owned_a, owned_b = fused(
        top_grad, layer_inputs[0], frozen[0], adapt_a[0], adapt_b[0], tenant_ids[None, :], owner_map
    )
    return grads[None], owned_a[None, None], owned_b[None, None]


def solution(mesh):
    return jax.shard_map(
        body,
        mesh=mesh,
        in_specs=(
            P("section", "dp", None),
            P("dp", None),
            P("dp"),
            P(),
            P("section", "dp", None),
            P("section", "dp", None),
            P("section", None, None),
        ),
        out_specs=(
            P("section", "dp", None),
            P("section", "dp", None, None),
            P("section", "dp", None, None),
        ),
        check_vma=False,
    )
```
